32 devices in a mesh: section: 4 (over x, core), space: 8 (over z, y).
Axes of the slice: x: 2, y: 2, z: 4, core: 2. Of those that a mesh axis runs over, the one named last changes fastest.
Arguments:
- features: bfloat16 [8, 2, 128, 1024], P(None, None, 'space'), may hold values from -6 to 6
- lift_w: bfloat16 [2, 32], replicated, may hold values from -4 to 4
- spec_w: bfloat16 [4, 64, 128, 32, 64], P('section', 'space'), may hold values from -3 to 3
- point_w: bfloat16 [4, 32, 32], P('section'), may hold values from -1.5 to 1.5
- point_b: bfloat16 [4, 32], P('section'), may hold values from -3 to 3
Outputs:
- saved: bfloat16 [4, 8, 32, 128, 1024], P('section', None, None, 'space')
The draws below stay inside these ranges and needn't reach their ends.
All inputs are finite; a program needn't handle non-finite values.
Results may differ from the reference program's by a relative error of at most 0.03.
Values may be sent and summed in bfloat16 or wider, within the bound.
No kernel may reach another device: no remote copies, remote signals or barrier semaphores. Data moves between devices by JAX's collectives and lax.ppermute only.
A program may use at most 128 MiB of HBM per device.

```python
import jax
import jax.numpy as jnp

CHANNELS = 32
COLS = 1024
MODES_W = 64
MODES_H = 128
FEATURES = 2
MICRO = 8
LAYERS = 4
ROWS = 128


def block_levels(rng, extent, pieces, smallest, high):
    def one(axis_at, parts):
        steps = jax.random.uniform(jax.random.fold_in(jax.random.fold_in(rng, 6), axis_at), (parts,), jnp.float32, smallest / len(pieces), high / len(pieces))
        return jnp.repeat(jnp.exp(steps), extent[axis_at] // parts).reshape((-1,) + (1,) * (len(extent) - axis_at - 1))

    loudness = one(*pieces[0])
    for cut in pieces[1:]:
        loudness = loudness * one(*cut)
    return loudness


def bell_draw(own_key, extent, width, limit, cuts=(), held_as=jnp.bfloat16):
    factor_of = block_levels(own_key, extent, cuts, -0.22, 0.18) if cuts else 1.0
    drawn = jax.random.normal(own_key, extent, jnp.float32) * width * factor_of
    return jnp.minimum(jnp.maximum(drawn, -limit), limit).astype(held_as)


def setup_inputs(seed: int = 0) -> dict:
    splits = jax.random.split(jax.random.key(seed), 6)
    return {
        "features": bell_draw(splits[0], (MICRO, FEATURES, ROWS, COLS), 1.0, 6.0, ((2, 8),)),
        "lift_w": bell_draw(splits[1], (FEATURES, CHANNELS), FEATURES ** -0.5, 4.0),
        "spec_w": bell_draw(splits[2], (LAYERS, MODES_W, MODES_H, CHANNELS, 2 * CHANNELS), 0.2, 3.0, ((0, 4), (1, 8))),
        "point_w": bell_draw(splits[3], (LAYERS, CHANNELS, CHANNELS), (CHANNELS // 2) ** -0.5, 1.5, ((0, 4),)),
        "point_b": bell_draw(splits[4], (LAYERS, CHANNELS), 0.5, 3.0, ((0, 4),)),
    }


def turn_table(first, second, period):
    product = (first[:, None] * second[None, :]) % period
    return 2.0 * jnp.pi * product.astype(jnp.float32) / period


def row_freqs(height, modes_h):
    index = jnp.arange(modes_h, dtype=jnp.int32)
    return jnp.where(index < modes_h // 2, index, height - modes_h + index).astype(jnp.int32)


def fwd_w_table(cols, modes_w):
    column = jnp.arange(cols, dtype=jnp.int32)
    slot = jnp.arange(2 * modes_w, dtype=jnp.int32)
    angle = turn_table(column, slot // 2, cols)
    return jnp.where(slot[None, :] % 2 == 0, jnp.cos(angle), -jnp.sin(angle)).astype(jnp.bfloat16)


def fwd_h_table(height, modes_h):
    angle = turn_table(jnp.arange(height, dtype=jnp.int32), row_freqs(height, modes_h), height)
    return jnp.concatenate([jnp.cos(angle), jnp.sin(angle)], axis=1).astype(jnp.bfloat16)


def inv_h_table(height, modes_h):
    angle = turn_table(row_freqs(height, modes_h), jnp.arange(height, dtype=jnp.int32), height)
    cosine = jnp.cos(angle) / height
    sine = jnp.sin(angle) / height
    upper = jnp.concatenate([cosine, sine], axis=1)
    lower = jnp.concatenate([-sine, cosine], axis=1)
    return jnp.concatenate([upper, lower], axis=0).astype(jnp.bfloat16)


def inv_w_table(cols, modes_w):
    slot = jnp.arange(2 * modes_w, dtype=jnp.int32)
    mode = slot // 2
    angle = turn_table(mode, jnp.arange(cols, dtype=jnp.int32), cols)
    factor = jnp.where(mode == 0, 1.0, 2.0).astype(jnp.float32)[:, None] / cols
    return jnp.where(slot[:, None] % 2 == 0, factor * jnp.cos(angle), -factor * jnp.sin(angle)).astype(jnp.bfloat16)


def one_layer(field, weights, gain_w, bias, tables):
    fw_tab, eh_tab, gi_tab, gw_tab = tables
    chans = field.shape[0]
    height = field.shape[1]
    modes_h = eh_tab.shape[1] // 2
    modes_w = fw_tab.shape[1] // 2
    upart = jnp.einsum("chw,wk->khc", field.astype(jnp.float32), fw_tab.astype(jnp.float32)).astype(jnp.bfloat16)
    proj = jnp.einsum("khc,hf->kcf", upart.astype(jnp.float32), eh_tab.astype(jnp.float32))
    proj = proj.reshape(modes_w, 2, chans, 2 * modes_h)
    spec_re = (proj[:, 0, :, :modes_h] + proj[:, 1, :, modes_h:]).astype(jnp.bfloat16)
    spec_im = (proj[:, 1, :, :modes_h] - proj[:, 0, :, modes_h:]).astype(jnp.bfloat16)
    wfloat = weights.astype(jnp.float32)
    mixed_re = jnp.einsum("jcf,jfco->jfo", spec_re.astype(jnp.float32), wfloat)
    mixed_im = jnp.einsum("jcf,jfco->jfo", spec_im.astype(jnp.float32), wfloat)
    out_re = (mixed_re[..., :chans] - mixed_im[..., chans:]).astype(jnp.bfloat16)
    out_im = (mixed_re[..., chans:] + mixed_im[..., :chans]).astype(jnp.bfloat16)
    stacked = jnp.stack([out_re, out_im], axis=1).reshape(modes_w, 2 * modes_h, chans)
    zpart = jnp.einsum("jmc,mn->jnc", stacked.astype(jnp.float32), gi_tab.astype(jnp.float32))
    zpart = zpart.reshape(2 * modes_w, height, chans).astype(jnp.bfloat16)
    spec = jnp.einsum("khc,kw->chw", zpart.astype(jnp.float32), gw_tab.astype(jnp.float32))
    point = jnp.einsum("chw,co->ohw", field.astype(jnp.float32), gain_w.astype(jnp.float32))
    point = point + bias.astype(jnp.float32)[:, None, None]
    return jax.nn.gelu(spec + point, approximate=True).astype(jnp.bfloat16)


def reference(features, lift_w, spec_w, point_w, point_b):
    tables = (fwd_w_table(COLS, MODES_W), fwd_h_table(ROWS, MODES_H), inv_h_table(ROWS, MODES_H), inv_w_table(COLS, MODES_W))
    results = []
    for micro_pos in range(MICRO):
        field = jnp.einsum("fhw,fc->chw", features[micro_pos].astype(jnp.float32), lift_w.astype(jnp.float32)).astype(jnp.bfloat16)
        layer_outs = []
        for layer_pos in range(LAYERS):
            field = one_layer(field, spec_w[layer_pos], point_w[layer_pos], point_b[layer_pos], tables)
            layer_outs.append(field)
        results.append(jnp.stack(layer_outs, axis=0))
    return jnp.stack(results, axis=1)
```

```python
import functools

import jax
import jax.numpy as jnp
import numpy as np
from jax import lax
from jax.experimental import pallas as pl
from jax.experimental.pallas import tpu as pltpu
from jax.sharding import PartitionSpec as P

BF16 = jnp.bfloat16
F32 = jnp.float32
BOTH = ("space", "section")


def turn_table(first, second, period):
    product = (first[:, None] * second[None, :]) % period
    return (np.float32(2.0 * np.pi) * product.astype(np.float32) / np.float32(period)).astype(np.float32)


def row_freqs(height, modes_h):
    index = np.arange(modes_h)
    return np.where(index < modes_h // 2, index, height - modes_h + index)


def mode_order(space, section, local, modes):
    part = np.arange(section)[None, None, :] * modes + np.arange(modes)[:, None, None]
    whole = np.arange(space)[None, :, None] * local + part
    return np.where(part < local, whole, -1).reshape(modes, space * section)


def swap_table(left, right, inner):
    size = left * right * inner
    target = np.arange(size).reshape(right, left, inner).transpose(1, 0, 2).reshape(-1)
    table = np.zeros((size, size), np.float32)
    table[np.arange(size), target] = 1.0
    return table.astype(BF16)


def fwd_w_table(cols, modes_w):
    slot = np.arange(2 * modes_w)
    angle = turn_table(np.arange(cols), slot // 2, cols)
    return np.where(slot[None, :] % 2 == 0, np.cos(angle), -np.sin(angle)).astype(BF16)


def fwd_h_table(height, modes_h):
    angle = turn_table(np.arange(height), row_freqs(height, modes_h), height)
    return np.concatenate([np.cos(angle), np.sin(angle)], axis=1).astype(BF16)


def inv_h_table(height, modes_h):
    angle = turn_table(row_freqs(height, modes_h), np.arange(height), height)
    cosine = np.cos(angle) / height
    sine = np.sin(angle) / height
    upper = np.concatenate([cosine, sine], axis=1)
    lower = np.concatenate([-sine, cosine], axis=1)
    return np.concatenate([upper, lower], axis=0).astype(BF16)


def inv_w_table(cols, modes_w):
    slot = np.arange(2 * modes_w)
    mode = slot // 2
    angle = turn_table(mode, np.arange(cols), cols)
    factor = np.where(mode == 0, 1.0, 2.0).astype(np.float32)[:, None] / cols
    return np.where(slot[:, None] % 2 == 0, factor * np.cos(angle), -factor * np.sin(angle)).astype(BF16)


def gelu(x):
    inner = x * (0.7978845608028654 + 0.035677408136300125 * (x * x))
    half = 0.5 * x
    return half + half * jnp.tanh(inner)


def dot(left, right):
    return jnp.dot(left, right, preferred_element_type=F32)


def dot_tn(left, right):
    return lax.dot_general(left, right, (((0,), (0,)), ((), ())), preferred_element_type=F32)


def dot_nt(left, right):
    return lax.dot_general(left, right, (((1,), (1,)), ((), ())), preferred_element_type=F32)


class Sizes:
    def __init__(self, space, section, rows, chans, own, modes, cols):
        self.space, self.section, self.rows, self.chans = space, section, rows, chans
        self.own, self.modes, self.cols = own, modes, cols
        self.devices = space * section
        self.micro = own * section
        self.flat = chans * rows
        self.chunk = min(rows, max(1, 128 // chans))
        self.turns = rows // self.chunk
        self.fwd = 2 * modes
        self.inv = own * modes
        self.slots = 2 * modes * self.devices


def build_mat(sz, layer, point_ref, expand_ref, mat_ref, bias_ref):
    pos = lax.axis_index("section")
    block = point_ref[pos ^ layer]
    weight = block[: sz.chans]
    spread = dot_nt(expand_ref[...], weight).astype(BF16)
    full = dot_nt(spread, expand_ref[...])
    row = lax.broadcasted_iota(jnp.int32, full.shape, 0) % sz.rows
    col = lax.broadcasted_iota(jnp.int32, full.shape, 1) % sz.rows
    mat_ref[...] = jnp.where(row == col, full, 0.0).astype(BF16)
    bias = jnp.broadcast_to(block[sz.chans : sz.chans + 1], (128, sz.chans))
    bias_ref[...] = dot_nt(expand_ref[...], bias)


def one_field(sz, z_ref, a_ref, mat_ref, bias_ref, gw_ref, out_ref):
    step = min(128, sz.flat)
    for start in range(0, sz.flat, step):
        rows = slice(start, start + step)
        value = dot(z_ref[rows, :], gw_ref[...]) + dot(mat_ref[rows, :], a_ref[...])
        out_ref[rows, :] = gelu(value + bias_ref[rows, :1]).astype(BF16)


def pack(sz, at, field_ref, fw_ref, order_ref, swap_ref, stage_ref, send_ref):
    count, wide = sz.devices, sz.chunk * sz.chans
    spectrum = dot(field_ref[...], fw_ref[...]).astype(BF16)
    turned = dot_tn(spectrum, order_ref[...]).astype(BF16)
    parts = []
    for t in range(sz.turns):
        lanes = slice(t * wide, (t + 1) * wide)
        parts.append(jnp.concatenate([turned[k * count : (k + 1) * count, lanes] for k in range(sz.fwd)], axis=1))
    moved = dot(jnp.concatenate(parts, axis=0), swap_ref[...])
    width = sz.fwd * sz.chans
    for t in range(sz.turns):
        for r in range(sz.chunk):
            place = (t * sz.chunk + r) * count
            stage_ref[place : place + count, :] = moved[t * count : (t + 1) * count, r * width : (r + 1) * width]
    for device in range(count):
        send_ref[device, at] = stage_ref[pl.ds(device, sz.rows, stride=count), :].astype(BF16)


def unpack(sz, back_ref, order_ref, swap_ref, stage_ref, turned_ref, z_ref):
    count, wide = sz.devices, sz.chunk * sz.chans
    width = sz.inv * sz.chans
    for q in range(2):
        for device in range(count):
            stage_ref[pl.ds(device, sz.rows, stride=count), :] = back_ref[device, q].astype(F32)
        parts = []
        for t in range(sz.turns):
            blocks = [
                stage_ref[(t * sz.chunk + r) * count : (t * sz.chunk + r + 1) * count, :] for r in range(sz.chunk)
            ]
            parts.append(jnp.concatenate(blocks, axis=1))
        moved = dot(jnp.concatenate(parts, axis=0).astype(BF16), swap_ref[...]).astype(BF16)
        for t in range(sz.turns):
            for k in range(sz.inv):
                m, mode = divmod(k, sz.modes)
                place = (q * sz.modes + mode) * count
                turned_ref[m, place : place + count, t * wide : (t + 1) * wide] = moved[
                    t * count : (t + 1) * count, k * wide : (k + 1) * wide
                ]
    for m in range(sz.own):
        z_ref[m] = dot_nt(order_ref[...], turned_ref[m]).astype(BF16)


def lift_kernel(sz, feat_ref, mat_ref, fw_ref, order_ref, swap_ref, out_ref, send_ref, stage_ref):
    out_ref[0] = dot(mat_ref[...], feat_ref[0]).astype(BF16)
    pack(sz, pl.program_id(0), out_ref.at[0], fw_ref, order_ref, swap_ref, stage_ref, send_ref)


def lift_rest_kernel(feat_ref, mat_ref, out_ref):
    out_ref[0] = dot(mat_ref[...], feat_ref[0]).astype(BF16)


def own_kernel(sz, layer, back_ref, a_ref, point_ref, expand_ref, order_ref, swap_i_ref, swap_f_ref, gw_ref, fw_ref,
               out_ref, z_ref, send_ref, mat_ref, bias_ref, stage_i_ref, stage_f_ref, turned_ref):
    at = pl.program_id(0)

    @pl.when(at == 0)
    def _():
        build_mat(sz, layer, point_ref, expand_ref, mat_ref, bias_ref)
        unpack(sz, back_ref, order_ref, swap_i_ref, stage_i_ref, turned_ref, z_ref)

    one_field(sz, z_ref.at[at], a_ref.at[0], mat_ref, bias_ref, gw_ref, out_ref.at[0])
    pack(sz, at, out_ref.at[0], fw_ref, order_ref, swap_f_ref, stage_f_ref, send_ref)


def unpack_kernel(sz, back_ref, order_ref, swap_ref, z_ref, stage_ref, turned_ref):
    unpack(sz, back_ref, order_ref, swap_ref, stage_ref, turned_ref, z_ref)


def run_fields(sz, jobs, mat_ref, bias_ref, gw_ref, in_ref, out_ref, in_sem, out_sem):
    loads = [pltpu.make_async_copy(job[1], in_ref.at[i % 2], in_sem.at[i % 2]) for i, job in enumerate(jobs)]
    stores = [pltpu.make_async_copy(out_ref.at[i % 2], job[2], out_sem.at[i % 2]) for i, job in enumerate(jobs)]
    loads[0].start()
    for i, job in enumerate(jobs):
        if i + 1 < len(jobs):
            loads[i + 1].start()
        loads[i].wait()
        if i >= 2:
            stores[i - 2].wait()
        if job[0] is None:
            out_ref[i % 2] = in_ref[i % 2]
        else:
            one_field(sz, job[0], in_ref.at[i % 2], mat_ref, bias_ref, gw_ref, out_ref.at[i % 2])
        stores[i].start()
    for store in stores[-2:]:
        store.wait()


def rest_kernel(sz, layer, *refs):
    z_refs = refs[: sz.section - 1]
    a_ref, point_ref, expand_ref, gw_ref, out_ref = refs[sz.section - 1 : sz.section + 4]
    mat_ref, bias_ref, in_ref, held_ref, in_sem, out_sem = refs[sz.section + 4 :]
    build_mat(sz, layer, point_ref, expand_ref, mat_ref, bias_ref)
    jobs = []
    for step in range(1, sz.section):
        for m in range(sz.own):
            at = (step - 1) * sz.own + m
            jobs.append((z_refs[step - 1].at[m], a_ref.at[at], out_ref.at[at]))
    run_fields(sz, jobs, mat_ref, bias_ref, gw_ref, in_ref, held_ref, in_sem, out_sem)


def final_kernel(sz, *refs):
    count = sz.section
    z_refs = refs[:count]
    fields = refs[count : 3 * count - 2]
    point_ref, expand_ref, gw_ref, out_ref = refs[3 * count - 2 : 3 * count + 2]
    mat_ref, bias_ref, in_ref, held_ref, in_sem, out_sem = refs[3 * count + 2 :]
    pos = lax.axis_index("section")

    def jobs_of(layer, with_z):
        source = min(layer, count - 2)
        mine, rest = fields[2 * source], fields[2 * source + 1]
        jobs = []
        for step in range(count):
            for m in range(sz.own):
                place = rest.at[(step - 1) * sz.own + m] if step else mine.at[m]
                z = z_refs[step].at[m] if with_z else None
                jobs.append((z, place, out_ref.at[(layer ^ step) * sz.own + m]))
        return jobs

    for layer in range(count - 1):

        @pl.when(pos == layer)
        def _():
            run_fields(sz, jobs_of(layer, False), mat_ref, bias_ref, gw_ref, in_ref, held_ref, in_sem, out_sem)

    @pl.when(pos == count - 1)
    def _():
        build_mat(sz, count - 1, point_ref, expand_ref, mat_ref, bias_ref)
        run_fields(sz, jobs_of(count - 1, True), mat_ref, bias_ref, gw_ref, in_ref, held_ref, in_sem, out_sem)


def mix_kernel(sz, layer, recv_ref, eh_ref, git_ref, *rest):
    w_refs = rest[: sz.section]
    out_ref, x_ref, w_ref, y_ref, sem = rest[sz.section :]
    pos = lax.axis_index("section")
    for step in range(sz.section):

        @pl.when(pos == (layer ^ step))
        def _():
            pltpu.make_async_copy(w_refs[step], w_ref, sem).start()

    modes_h = eh_ref.shape[1] // 2
    chans = sz.chans
    for src in range(sz.section):
        for m in range(sz.own):
            cols = recv_ref[:, src, m].reshape(sz.space * sz.rows, sz.fwd * chans)
            proj = dot_tn(cols, eh_ref[...])
            for mode in range(sz.modes):
                real = proj[2 * mode * chans : (2 * mode + 1) * chans]
                imag = proj[(2 * mode + 1) * chans : (2 * mode + 2) * chans]
                x_ref[mode, src * sz.own + m, 0] = real[:, :modes_h] + imag[:, modes_h:]
                x_ref[mode, src * sz.own + m, 1] = imag[:, :modes_h] - real[:, modes_h:]
    pltpu.make_async_copy(w_refs[0], w_ref, sem).wait()
    group = min(4, sz.micro)
    for mode in range(sz.modes):
        for base in range(0, sz.micro, group):

            def body(c, accs):
                weight = w_ref[mode, c].astype(F32)
                w_re = weight[:chans]
                w_im = weight[chans:]
                new = []
                for g in range(group):
                    x_re = x_ref[mode, base + g, 0, pl.ds(c, 1), :]
                    x_im = x_ref[mode, base + g, 1, pl.ds(c, 1), :]
                    re, im = accs[2 * g], accs[2 * g + 1]
                    new.append(re + (x_re * w_re - x_im * w_im))
                    new.append(im + (x_re * w_im + x_im * w_re))
                return tuple(new)

            zero = jnp.zeros((chans, modes_h), F32)
            accs = lax.fori_loop(0, chans, body, (zero,) * (2 * group), unroll=4)
            for g in range(group):
                at = ((base + g) * sz.modes + mode) * chans
                y_ref[at : at + chans, :modes_h] = accs[2 * g].astype(BF16)
                y_ref[at : at + chans, modes_h:] = accs[2 * g + 1].astype(BF16)
    back = dot_nt(git_ref[...], y_ref[...]).astype(BF16)
    lanes = sz.inv * chans
    height = sz.space * sz.rows
    for sp in range(sz.space):
        for dest in range(sz.section):
            for q in range(2):
                start = q * height + sp * sz.rows
                out_ref[sp, dest, q] = back[start : start + sz.rows, dest * lanes : (dest + 1) * lanes]


def whole_block(array):
    zeros = (0,) * array.ndim
    return pl.BlockSpec(array.shape, lambda i: zeros)


def one_block(shape):
    zeros = (0,) * (len(shape) - 1)
    return pl.BlockSpec((1,) + tuple(shape[1:]), lambda i: (i,) + zeros)


ANY = pl.BlockSpec(memory_space=pl.ANY)
VMEM = pl.BlockSpec(memory_space=pltpu.VMEM)


def params(size=56):
    return pltpu.CompilerParams(vmem_limit_bytes=size * 1024 * 1024)


def cost(sz, fields, extra=0):
    return pl.CostEstimate(
        flops=fields * 2 * sz.flat * sz.cols * (sz.flat + 256) + extra,
        bytes_accessed=fields * 4 * sz.flat * sz.cols,
        transcendentals=fields * sz.flat * sz.cols,
    )


def shape_of(*shape, dtype=BF16):
    return jax.ShapeDtypeStruct(shape, dtype)


def stage_f(sz):
    return pltpu.VMEM((sz.rows * sz.devices, sz.fwd * sz.chans), F32)


def stage_i(sz):
    return pltpu.VMEM((sz.rows * sz.devices, sz.inv * sz.chans), F32)


def turned(sz):
    return pltpu.VMEM((sz.own, sz.slots, sz.flat), BF16)


def mats(sz):
    return [pltpu.VMEM((sz.flat, sz.flat), BF16), pltpu.VMEM((sz.flat, 128), F32)]


def send_shape(sz):
    return shape_of(sz.devices, sz.own, sz.rows, sz.fwd * sz.chans)


def streams(sz):
    return [
        pltpu.VMEM((2, sz.flat, sz.cols), BF16),
        pltpu.VMEM((2, sz.flat, sz.cols), BF16),
        pltpu.SemaphoreType.DMA((2,)),
        pltpu.SemaphoreType.DMA((2,)),
    ]


def call_lift(sz, feat, mat, tabs):
    outs = [shape_of(sz.own, sz.flat, sz.cols), send_shape(sz)]
    args = (feat, mat, tabs["fw"], tabs["order"], tabs["swap_f"])
    return pl.pallas_call(
        functools.partial(lift_kernel, sz),
        grid=(sz.own,),
        in_specs=[one_block(feat.shape)] + [whole_block(a) for a in args[1:]],
        out_specs=[one_block(outs[0].shape), whole_block(outs[1])],
        out_shape=outs,
        scratch_shapes=[stage_f(sz)],
        compiler_params=params(),
        cost_estimate=cost(sz, sz.own),
        name="lift",
    )(*args)


def call_lift_rest(sz, feat, mat):
    out = shape_of(feat.shape[0], sz.flat, sz.cols)
    return pl.pallas_call(
        lift_rest_kernel,
        grid=(feat.shape[0],),
        in_specs=[one_block(feat.shape), whole_block(mat)],
        out_specs=one_block(out.shape),
        out_shape=out,
        compiler_params=params(),
        cost_estimate=cost(sz, feat.shape[0]),
        name="lift_rest",
    )(feat, mat)


def call_own(sz, layer, back, a, point, tabs):
    outs = [shape_of(*a.shape), shape_of(sz.own, sz.flat, sz.slots), send_shape(sz)]
    args = (back, a, point, tabs["expand"], tabs["order"], tabs["swap_i"], tabs["swap_f"], tabs["gw"], tabs["fw"])
    return pl.pallas_call(
        functools.partial(own_kernel, sz, layer),
        grid=(sz.own,),
        in_specs=[whole_block(back), one_block(a.shape)] + [whole_block(x) for x in args[2:]],
        out_specs=[one_block(outs[0].shape), whole_block(outs[1]), whole_block(outs[2])],
        out_shape=outs,
        scratch_shapes=mats(sz) + [stage_i(sz), stage_f(sz), turned(sz)],
        compiler_params=params(),
        cost_estimate=cost(sz, sz.own),
        name="own_field",
    )(*args)


def call_unpack(sz, back, tabs):
    return pl.pallas_call(
        functools.partial(unpack_kernel, sz),
        in_specs=[VMEM] * 3,
        out_specs=VMEM,
        out_shape=shape_of(sz.own, sz.flat, sz.slots),
        scratch_shapes=[stage_i(sz), turned(sz)],
        compiler_params=params(),
        cost_estimate=cost(sz, 1),
        name="unpack",
    )(back, tabs["order"], tabs["swap_i"])


def call_rest(sz, layer, zs, a, point, tabs):
    return pl.pallas_call(
        functools.partial(rest_kernel, sz, layer),
        in_specs=[VMEM] * len(zs) + [ANY, VMEM, VMEM, VMEM],
        out_specs=ANY,
        out_shape=shape_of(*a.shape),
        scratch_shapes=mats(sz) + streams(sz),
        compiler_params=params(),
        cost_estimate=cost(sz, a.shape[0]),
        name="rest_fields",
    )(*zs, a, point, tabs["expand"], tabs["gw"])


def call_final(sz, zs, fields, point, tabs):
    return pl.pallas_call(
        functools.partial(final_kernel, sz),
        in_specs=[VMEM] * len(zs) + [ANY] * len(fields) + [VMEM, VMEM, VMEM],
        out_specs=ANY,
        out_shape=shape_of(sz.micro, sz.flat, sz.cols),
        scratch_shapes=mats(sz) + streams(sz),
        compiler_params=params(),
        cost_estimate=cost(sz, sz.micro),
        name="final_fields",
    )(*zs, *fields, point, tabs["expand"], tabs["gw"])


def call_mix(sz, layer, recv, weights, tabs):
    modes_h = tabs["eh"].shape[1] // 2
    return pl.pallas_call(
        functools.partial(mix_kernel, sz, layer),
        in_specs=[VMEM, VMEM, VMEM] + [ANY] * sz.section,
        out_specs=VMEM,
        out_shape=shape_of(sz.space, sz.section, 2, sz.rows, sz.inv * sz.chans),
        scratch_shapes=[
            pltpu.VMEM((sz.modes, sz.micro, 2, sz.chans, modes_h), F32),
            pltpu.VMEM(weights[0].shape, BF16),
            pltpu.VMEM((sz.micro * sz.modes * sz.chans, 2 * modes_h), BF16),
            pltpu.SemaphoreType.DMA,
        ],
        compiler_params=params(),
        cost_estimate=pl.CostEstimate(flops=4_000_000_000, bytes_accessed=2_000_000, transcendentals=0),
        name="mix",
    )(recv, tabs["eh"], tabs["git"], *weights)


def exchange(value, count):
    return lax.all_to_all(value, BOTH, split_axis=0, concat_axis=0, tiled=True)


def swap(value, step, count, parity=None):
    pairs = [(i, i ^ step) for i in range(count) if parity is None or i % 2 == parity]
    return lax.ppermute(value, "section", pairs)


def on_device(features, lift_w, spec_w, point_w, point_b):
    space = lax.axis_size("space")
    section = lax.axis_size("section")
    pos = lax.axis_index("section")
    micro, feats, rows, cols = features.shape
    chans = lift_w.shape[1]
    local = spec_w.shape[1]
    modes_h = spec_w.shape[2]
    modes_w = local * space
    height = rows * space
    modes = -(-local // section)
    spare = modes * section - local
    sz = Sizes(space, section, rows, chans, micro // section, modes, cols)

    order = mode_order(space, section, local, modes)
    known = (order >= 0)[:, None, :]
    slot = np.stack([2 * order, 2 * order + 1], axis=1) * known
    fw = np.where(known.reshape(1, modes, 1, -1), fwd_w_table(cols, modes_w).astype(np.float32)[:, slot], 0.0)
    gw = np.where(known[..., None], inv_w_table(cols, modes_w).astype(np.float32)[slot], 0.0)
    gw = gw.transpose(1, 0, 2, 3).reshape(sz.slots, cols)
    tabs = {
        "fw": fw.reshape(cols, sz.slots).astype(BF16),
        "gw": gw.astype(BF16),
        "eh": fwd_h_table(height, modes_h),
        "git": np.ascontiguousarray(inv_h_table(height, modes_h).T),
        "order": swap_table(chans, rows, 1),
        "swap_f": swap_table(sz.fwd, sz.chunk, chans),
        "swap_i": swap_table(sz.chunk, sz.inv, chans),
        "expand": np.repeat(np.eye(chans, dtype=np.float32), rows, axis=0).astype(BF16),
    }
    tabs = {name: jnp.asarray(table) for name, table in tabs.items()}

    point = jnp.concatenate([point_w[0], point_b, jnp.zeros((7, chans), BF16)], axis=0)
    point = jnp.stack([point] + [swap(point, d, section) for d in range(1, section)], axis=0)

    weights = spec_w[0].transpose(0, 2, 3, 1)
    weights = jnp.pad(weights, ((0, spare), (0, 0), (0, 0), (0, 0)))
    weights = weights.reshape((section, modes) + weights.shape[1:])
    parts = [lax.dynamic_index_in_dim(weights, pos ^ d, 0, keepdims=False) for d in range(section)]
    near = swap(parts[1], 1, section)
    even = [parts[0], near] + [swap(parts[d], d, section, 0) for d in range(2, section)]
    odd = [parts[0], near] + [swap(parts[d], d, section, 1) for d in range(2, section)]

    lift_mat = jnp.einsum("fc,rs->crfs", lift_w, jnp.eye(rows, dtype=BF16)).reshape(sz.flat, feats * rows)
    flat = features.reshape(section, sz.own, feats * rows, cols)
    feat = [lax.dynamic_index_in_dim(flat, pos ^ d, 0, keepdims=False) for d in range(section)]
    field, send = call_lift(sz, feat[0], lift_mat, tabs)
    rest = call_lift_rest(sz, jnp.concatenate(feat[1:], axis=0), lift_mat)

    fields = []
    for layer in range(section):
        recv = exchange(send, sz.devices).reshape(space, section, sz.own, rows, sz.fwd * chans)
        back = call_mix(sz, layer, recv, odd if layer % 2 else even, tabs)
        back = exchange(back.reshape(sz.devices, 2, rows, sz.inv * chans), sz.devices)
        if layer + 1 < section:
            field, z, send = call_own(sz, layer, back, field, point, tabs)
            rest = call_rest(sz, layer, [swap(z, d, section) for d in range(1, section)], rest, point, tabs)
            fields += [field, rest]
        else:
            z = call_unpack(sz, back, tabs)
            zs = [z] + [swap(z, d, section) for d in range(1, section)]
            out = call_final(sz, zs, fields, point, tabs)
    return out.reshape(1, micro, chans, rows, cols)


def solution(mesh):
    in_specs = (
        P(None, None, "space", None),
        P(),
        P("section", "space", None, None, None),
        P("section", None, None),
        P("section", None),
    )
    out_specs = P("section", None, None, "space", None)
    return jax.shard_map(on_device, mesh=mesh, in_specs=in_specs, out_specs=out_specs, check_vma=False)
```

```python
import functools

import jax
import jax.numpy as jnp
import numpy as np
from jax import lax
from jax.experimental import pallas as pl
from jax.experimental.pallas import tpu as pltpu
from jax.sharding import PartitionSpec as P

BF16 = jnp.bfloat16
F32 = jnp.float32
BOTH = ("space", "section")


def turn_table(first, second, period):
    product = (first[:, None] * second[None, :]) % period
    return (np.float32(2.0 * np.pi) * product.astype(np.float32) / np.float32(period)).astype(np.float32)


def row_freqs(height, modes_h):
    index = np.arange(modes_h)
    return np.where(index < modes_h // 2, index, height - modes_h + index)


def mode_order(space, section, local, modes):
    part = np.arange(section)[None, None, :] * modes + np.arange(modes)[:, None, None]
    whole = np.arange(space)[None, :, None] * local + part
    return np.where(part < local, whole, -1).reshape(modes, space * section)


def fwd_w_table(cols, modes_w):
    slot = np.arange(2 * modes_w)
    angle = turn_table(np.arange(cols), slot // 2, cols)
    return np.where(slot[None, :] % 2 == 0, np.cos(angle), -np.sin(angle)).astype(BF16)


def fwd_h_table(height, modes_h):
    angle = turn_table(np.arange(height), row_freqs(height, modes_h), height)
    return np.concatenate([np.cos(angle), np.sin(angle)], axis=1).astype(BF16)


def inv_h_table(height, modes_h):
    angle = turn_table(row_freqs(height, modes_h), np.arange(height), height)
    cosine = np.cos(angle) / height
    sine = np.sin(angle) / height
    upper = np.concatenate([cosine, sine], axis=1)
    lower = np.concatenate([-sine, cosine], axis=1)
    return np.concatenate([upper, lower], axis=0).astype(BF16)


def inv_w_table(cols, modes_w):
    slot = np.arange(2 * modes_w)
    mode = slot // 2
    angle = turn_table(mode, np.arange(cols), cols)
    factor = np.where(mode == 0, 1.0, 2.0).astype(np.float32)[:, None] / cols
    return np.where(slot[:, None] % 2 == 0, factor * np.cos(angle), -factor * np.sin(angle)).astype(BF16)


def gelu(half):
    half = half.astype(BF16)
    inner = half * (BF16(1.5957691216057308) + BF16(0.2854192650890401) * (half * half))
    return half + half * jnp.tanh(inner)


def dot(left, right):
    return jnp.dot(left, right, preferred_element_type=F32)


def dot_tn(left, right):
    return lax.dot_general(left, right, (((0,), (0,)), ((), ())), preferred_element_type=F32)


def dot_nt(left, right):
    return lax.dot_general(left, right, (((1,), (1,)), ((), ())), preferred_element_type=F32)


class Sizes:
    def __init__(self, space, section, rows, chans, own, modes, cols):
        self.space, self.section, self.rows, self.chans = space, section, rows, chans
        self.own, self.modes, self.cols = own, modes, cols
        self.devices = space * section
        self.micro = own * section
        self.flat = chans * rows
        self.chunk = min(rows, max(1, 128 // chans))
        self.turns = rows // self.chunk
        self.fwd = 2 * modes
        self.inv = own * modes
        self.slots = 2 * modes * self.devices


def iota(shape, axis):
    return lax.broadcasted_iota(jnp.int32, shape, axis)


def build_swap(ref, left, right, inner):
    size = left * right * inner
    row = iota((size, 1), 0)
    first, second, third = row // (right * inner), row // inner % right, row % inner
    target = (second * left + first) * inner + third
    ref[...] = jnp.where(iota((size, size), 1) == target, 1.0, 0.0).astype(BF16)


def build_mat(sz, layer, point_ref, mat_ref, bias_ref):
    pos = lax.axis_index("section")
    block = point_ref[pos ^ layer] * BF16(0.5)
    expand = jnp.where(iota((sz.flat, sz.chans), 0) // sz.rows == iota((sz.flat, sz.chans), 1), 1.0, 0.0).astype(BF16)
    spread = dot_nt(expand, block[: sz.chans]).astype(BF16)
    full = dot_nt(spread, expand)
    same = iota((sz.flat, 1), 0) % sz.rows == iota((1, sz.flat), 1) % sz.rows
    mat_ref[...] = jnp.where(same, full, 0.0).astype(BF16)
    bias = jnp.broadcast_to(block[sz.chans : sz.chans + 1], (128, sz.chans))
    bias = jnp.where(iota(bias.shape, 0) == 0, bias.astype(F32), 0.0).astype(BF16)
    bias_ref[...] = dot_nt(expand, bias).astype(BF16)


def one_field(sz, z_ref, a_ref, mat_ref, bias_ref, gw_ref, out_ref):
    step = min(512, sz.cols)
    left = jnp.concatenate([mat_ref[...], z_ref[...], bias_ref[...]], axis=1)
    ones = jnp.ones((128, step), BF16)
    for start in range(0, sz.cols, step):
        cols = slice(start, start + step)
        right = jnp.concatenate([a_ref[:, cols], gw_ref[:, cols], ones], axis=0)
        out_ref[:, cols] = gelu(dot(left, right))


def pack(sz, at, field_ref, fw_ref, order_ref, swap_ref, stage_ref, send_ref):
    count, wide = sz.devices, sz.chunk * sz.chans
    spectrum = dot(field_ref[...], fw_ref[...]).astype(BF16)
    turned = dot_tn(spectrum, order_ref[...]).astype(BF16)
    parts = []
    for t in range(sz.turns):
        lanes = slice(t * wide, (t + 1) * wide)
        parts.append(jnp.concatenate([turned[k * count : (k + 1) * count, lanes] for k in range(sz.fwd)], axis=1))
    moved = dot(jnp.concatenate(parts, axis=0), swap_ref[...])
    width = sz.fwd * sz.chans
    for t in range(sz.turns):
        for r in range(sz.chunk):
            place = (t * sz.chunk + r) * count
            stage_ref[place : place + count, :] = moved[t * count : (t + 1) * count, r * width : (r + 1) * width]
    for device in range(count):
        send_ref[device, at] = stage_ref[pl.ds(device, sz.rows, stride=count), :].astype(BF16)


def unpack(sz, back_ref, order_ref, swap_ref, stage_ref, turned_ref, z_ref):
    count, wide = sz.devices, sz.chunk * sz.chans
    width = sz.inv * sz.chans
    for q in range(2):
        for device in range(count):
            stage_ref[pl.ds(device, sz.rows, stride=count), :] = back_ref[device, q].astype(F32)
        parts = []
        for t in range(sz.turns):
            blocks = [
                stage_ref[(t * sz.chunk + r) * count : (t * sz.chunk + r + 1) * count, :] for r in range(sz.chunk)
            ]
            parts.append(jnp.concatenate(blocks, axis=1))
        moved = dot(jnp.concatenate(parts, axis=0).astype(BF16), swap_ref[...]).astype(BF16)
        for t in range(sz.turns):
            for k in range(sz.inv):
                m, mode = divmod(k, sz.modes)
                place = (q * sz.modes + mode) * count
                turned_ref[m, place : place + count, t * wide : (t + 1) * wide] = moved[
                    t * count : (t + 1) * count, k * wide : (k + 1) * wide
                ]
    for m in range(sz.own):
        z_ref[m] = dot_nt(order_ref[...], turned_ref[m]).astype(BF16)


def copy_in(source, target, sem):
    copy = pltpu.make_async_copy(source, target, sem)
    copy.start()
    return copy


def lift_kernel(sz, feat_ref, mat_ref, fw_hbm, out_ref, send_ref, *scratch):
    fw_ref, order_ref, swap_ref, stage_ref, held_ref, in_sem, out_sem = scratch
    load = copy_in(fw_hbm, fw_ref, in_sem.at[0])
    build_swap(order_ref, sz.chans, sz.rows, 1)
    build_swap(swap_ref, sz.fwd, sz.chunk, sz.chans)
    stores = []
    for m in range(sz.own):
        held_ref[m] = dot(mat_ref[...], feat_ref[m]).astype(BF16)
        stores.append(copy_in(held_ref.at[m], out_ref.at[m], out_sem.at[m]))
        if m == 0:
            load.wait()
        pack(sz, m, held_ref.at[m], fw_ref, order_ref, swap_ref, stage_ref, send_ref)
    for store in stores:
        store.wait()


def lift_rest_kernel(sz, feat_ref, mat_ref, out_ref, held_ref, out_sem):
    stores = []
    for i in range(feat_ref.shape[0]):
        if i >= 2:
            stores[i - 2].wait()
        held_ref[i % 2] = dot(mat_ref[...], feat_ref[i]).astype(BF16)
        stores.append(copy_in(held_ref.at[i % 2], out_ref.at[i], out_sem.at[i % 2]))
    for store in stores[-2:]:
        store.wait()


def own_kernel(sz, layer, back_ref, a_hbm, point_ref, gw_hbm, fw_hbm, out_ref, z_ref, send_ref, *scratch):
    (mat_ref, bias_ref, in_ref, held_ref, in_sem, out_sem, gw_ref, tab_sem,
     fw_ref, order_ref, swap_f_ref, swap_i_ref, stage_f_ref, stage_i_ref, turned_ref) = scratch
    gw_load = copy_in(gw_hbm, gw_ref, tab_sem.at[0])
    loads = [copy_in(a_hbm.at[m], in_ref.at[m], in_sem.at[m]) for m in range(sz.own)]
    fw_load = copy_in(fw_hbm, fw_ref, tab_sem.at[1])
    build_swap(order_ref, sz.chans, sz.rows, 1)
    build_swap(swap_i_ref, sz.chunk, sz.inv, sz.chans)
    build_swap(swap_f_ref, sz.fwd, sz.chunk, sz.chans)
    build_mat(sz, layer, point_ref, mat_ref, bias_ref)
    unpack(sz, back_ref, order_ref, swap_i_ref, stage_i_ref, turned_ref, z_ref)
    gw_load.wait()
    stores = []
    for m in range(sz.own):
        loads[m].wait()
        one_field(sz, z_ref.at[m], in_ref.at[m], mat_ref, bias_ref, gw_ref, held_ref.at[m])
        stores.append(copy_in(held_ref.at[m], out_ref.at[m], out_sem.at[m]))
        if m == 0:
            fw_load.wait()
        pack(sz, m, held_ref.at[m], fw_ref, order_ref, swap_f_ref, stage_f_ref, send_ref)
    for store in stores:
        store.wait()


def unpack_kernel(sz, back_ref, z_ref, order_ref, swap_ref, stage_ref, turned_ref):
    build_swap(order_ref, sz.chans, sz.rows, 1)
    build_swap(swap_ref, sz.chunk, sz.inv, sz.chans)
    unpack(sz, back_ref, order_ref, swap_ref, stage_ref, turned_ref, z_ref)


def run_fields(sz, layer, jobs, point_ref, gw_hbm, scratch):
    mat_ref, bias_ref, in_ref, held_ref, in_sem, out_sem, gw_ref, tab_sem = scratch
    gw_load = copy_in(gw_hbm, gw_ref, tab_sem.at[0])
    loads = [copy_in(job[1], in_ref.at[i], in_sem.at[i]) for i, job in enumerate(jobs)]
    build_mat(sz, layer, point_ref, mat_ref, bias_ref)
    gw_load.wait()
    stores = []
    for i, (z_ref, _, target) in enumerate(jobs):
        loads[i].wait()
        if i >= 2:
            stores[i - 2].wait()
        one_field(sz, z_ref, in_ref.at[i], mat_ref, bias_ref, gw_ref, held_ref.at[i % 2])
        stores.append(copy_in(held_ref.at[i % 2], target, out_sem.at[i % 2]))
    for store in stores[-2:]:
        store.wait()


def run_copies(jobs, scratch):
    _, _, in_ref, _, in_sem, out_sem, _, _ = scratch
    loads = [copy_in(source, in_ref.at[i], in_sem.at[i]) for i, (source, _) in enumerate(jobs)]
    stores = []
    for i, (_, target) in enumerate(jobs):
        loads[i].wait()
        stores.append(copy_in(in_ref.at[i], target, out_sem.at[i]))
    for store in stores:
        store.wait()


def rest_kernel(sz, layer, *refs):
    z_refs = refs[: sz.section - 1]
    a_ref, point_ref, gw_hbm, out_ref = refs[sz.section - 1 : sz.section + 3]
    jobs = []
    for step in range(1, sz.section):
        for m in range(sz.own):
            at = (step - 1) * sz.own + m
            jobs.append((z_refs[step - 1].at[m], a_ref.at[at], out_ref.at[at]))
    run_fields(sz, layer, jobs, point_ref, gw_hbm, refs[sz.section + 3 :])


def final_own_kernel(sz, z_ref, *refs):
    count = sz.section
    fields = refs[: 2 * count - 2]
    point_ref, gw_hbm, out_ref = refs[2 * count - 2 : 2 * count + 1]
    scratch = refs[2 * count + 1 :]
    pos = lax.axis_index("section")
    for layer in range(count - 1):

        @pl.when(pos == layer)
        def _():
            jobs = []
            for step in range(count):
                for m in range(sz.own):
                    place = fields[2 * layer + 1].at[(step - 1) * sz.own + m] if step else fields[2 * layer].at[m]
                    jobs.append((place, out_ref.at[(layer ^ step) * sz.own + m]))
            run_copies(jobs, scratch)

    @pl.when(pos == count - 1)
    def _():
        mine = fields[2 * count - 4]
        jobs = [(z_ref.at[m], mine.at[m], out_ref.at[(count - 1) * sz.own + m]) for m in range(sz.own)]
        run_fields(sz, count - 1, jobs, point_ref, gw_hbm, scratch)


def final_rest_kernel(sz, steps, *refs):
    z_refs = refs[: len(steps)]
    _, rest_ref, point_ref, gw_hbm, out_ref = refs[len(steps) : len(steps) + 5]
    last = sz.section - 1

    @pl.when(lax.axis_index("section") == last)
    def _():
        jobs = []
        for z_ref, step in zip(z_refs, steps):
            for m in range(sz.own):
                target = out_ref.at[(last ^ step) * sz.own + m]
                jobs.append((z_ref.at[m], rest_ref.at[(step - 1) * sz.own + m], target))
        run_fields(sz, last, jobs, point_ref, gw_hbm, refs[len(steps) + 5 :])


def mix_kernel(sz, layer, recv_ref, eh_ref, git_ref, *rest):
    w_refs = rest[: sz.section]
    out_ref, x_ref, w_ref, y_ref, sem = rest[sz.section :]
    pos = lax.axis_index("section")
    for step in range(sz.section):

        @pl.when(pos == (layer ^ step))
        def _():
            pltpu.make_async_copy(w_refs[step], w_ref, sem).start()

    modes_h = eh_ref.shape[1] // 2
    chans = sz.chans
    for src in range(sz.section):
        for m in range(sz.own):
            cols = recv_ref[:, src, m].reshape(sz.space * sz.rows, sz.fwd * chans)
            proj = dot_tn(cols, eh_ref[...])
            for mode in range(sz.modes):
                real = proj[2 * mode * chans : (2 * mode + 1) * chans]
                imag = proj[(2 * mode + 1) * chans : (2 * mode + 2) * chans]
                x_ref[mode, src * sz.own + m, 0] = real[:, :modes_h] + imag[:, modes_h:]
                x_ref[mode, src * sz.own + m, 1] = imag[:, :modes_h] - real[:, modes_h:]
    pltpu.make_async_copy(w_refs[0], w_ref, sem).wait()
    group = min(4, sz.micro)
    for mode in range(sz.modes):
        for base in range(0, sz.micro, group):

            def body(c, accs):
                weight = w_ref[mode, c].astype(F32)
                w_re = weight[:chans]
                w_im = weight[chans:]
                new = []
                for g in range(group):
                    x_re = x_ref[mode, base + g, 0, pl.ds(c, 1), :]
                    x_im = x_ref[mode, base + g, 1, pl.ds(c, 1), :]
                    re, im = accs[2 * g], accs[2 * g + 1]
                    new.append(re + (x_re * w_re - x_im * w_im))
                    new.append(im + (x_re * w_im + x_im * w_re))
                return tuple(new)

            zero = jnp.zeros((chans, modes_h), F32)
            accs = lax.fori_loop(0, chans, body, (zero,) * (2 * group), unroll=4)
            for g in range(group):
                at = ((base + g) * sz.modes + mode) * chans
                y_ref[at : at + chans, :modes_h] = accs[2 * g].astype(BF16)
                y_ref[at : at + chans, modes_h:] = accs[2 * g + 1].astype(BF16)
    back = dot_nt(git_ref[...], y_ref[...]).astype(BF16)
    lanes = sz.inv * chans
    height = sz.space * sz.rows
    for sp in range(sz.space):
        for dest in range(sz.section):
            for q in range(2):
                start = q * height + sp * sz.rows
                out_ref[sp, dest, q] = back[start : start + sz.rows, dest * lanes : (dest + 1) * lanes]


HBM = pl.BlockSpec(memory_space=pltpu.HBM)
VMEM = pl.BlockSpec(memory_space=pltpu.VMEM)


def params(size=52):
    return pltpu.CompilerParams(vmem_limit_bytes=size * 1024 * 1024)


def cost(sz, fields, extra=0):
    return pl.CostEstimate(
        flops=fields * 2 * sz.flat * sz.cols * (sz.flat + 256) + extra,
        bytes_accessed=fields * 4 * sz.flat * sz.cols,
        transcendentals=fields * sz.flat * sz.cols,
    )


def shape_of(*shape, dtype=BF16):
    return jax.ShapeDtypeStruct(shape, dtype)


def stage_f(sz):
    return pltpu.VMEM((sz.rows * sz.devices, sz.fwd * sz.chans), F32)


def stage_i(sz):
    return pltpu.VMEM((sz.rows * sz.devices, sz.inv * sz.chans), F32)


def turned(sz):
    return pltpu.VMEM((sz.own, sz.slots, sz.flat), BF16)


def send_shape(sz):
    return shape_of(sz.devices, sz.own, sz.rows, sz.fwd * sz.chans)


def square(*sizes):
    size = int(np.prod(sizes))
    return pltpu.VMEM((size, size), BF16)


def sems(count):
    return pltpu.SemaphoreType.DMA((count,))


def streams(sz, jobs):
    return [
        square(sz.flat),
        pltpu.VMEM((sz.flat, 128), BF16),
        pltpu.VMEM((jobs, sz.flat, sz.cols), BF16),
        pltpu.VMEM((2, sz.flat, sz.cols), BF16),
        sems(jobs),
        sems(jobs),
        pltpu.VMEM((sz.slots, sz.cols), BF16),
        sems(2),
    ]


def call_lift(sz, feat, mat, tabs):
    return pl.pallas_call(
        functools.partial(lift_kernel, sz),
        in_specs=[VMEM, VMEM, HBM],
        out_specs=[HBM, VMEM],
        out_shape=[shape_of(sz.own, sz.flat, sz.cols), send_shape(sz)],
        scratch_shapes=[
            pltpu.VMEM((sz.cols, sz.slots), BF16),
            square(sz.flat),
            square(sz.fwd, sz.chunk, sz.chans),
            stage_f(sz),
            pltpu.VMEM((sz.own, sz.flat, sz.cols), BF16),
            sems(1),
            sems(sz.own),
        ],
        compiler_params=params(),
        cost_estimate=cost(sz, sz.own),
        name="lift",
    )(feat, mat, tabs["fw"])


def call_lift_rest(sz, feat, mat):
    return pl.pallas_call(
        functools.partial(lift_rest_kernel, sz),
        in_specs=[VMEM, VMEM],
        out_specs=HBM,
        out_shape=shape_of(feat.shape[0], sz.flat, sz.cols),
        scratch_shapes=[pltpu.VMEM((2, sz.flat, sz.cols), BF16), sems(2)],
        compiler_params=params(),
        cost_estimate=cost(sz, feat.shape[0]),
        name="lift_rest",
    )(feat, mat)


def call_own(sz, layer, back, a, point, tabs):
    return pl.pallas_call(
        functools.partial(own_kernel, sz, layer),
        in_specs=[VMEM, HBM, VMEM, HBM, HBM],
        out_specs=[HBM, VMEM, VMEM],
        out_shape=[shape_of(*a.shape), shape_of(sz.own, sz.flat, sz.slots), send_shape(sz)],
        scratch_shapes=streams(sz, max(sz.own, 2))
        + [
            pltpu.VMEM((sz.cols, sz.slots), BF16),
            square(sz.flat),
            square(sz.fwd, sz.chunk, sz.chans),
            square(sz.inv, sz.chunk, sz.chans),
            stage_f(sz),
            stage_i(sz),
            turned(sz),
        ],
        compiler_params=params(),
        cost_estimate=cost(sz, sz.own),
        name="own_field",
    )(back, a, point, tabs["gw"], tabs["fw"])


def call_unpack(sz, back):
    return pl.pallas_call(
        functools.partial(unpack_kernel, sz),
        in_specs=[VMEM],
        out_specs=VMEM,
        out_shape=shape_of(sz.own, sz.flat, sz.slots),
        scratch_shapes=[square(sz.flat), square(sz.inv, sz.chunk, sz.chans), stage_i(sz), turned(sz)],
        compiler_params=params(),
        cost_estimate=cost(sz, 1),
        name="unpack",
    )(back)


def call_rest(sz, layer, zs, a, point, tabs):
    return pl.pallas_call(
        functools.partial(rest_kernel, sz, layer),
        in_specs=[VMEM] * len(zs) + [HBM, VMEM, HBM],
        out_specs=HBM,
        out_shape=shape_of(*a.shape),
        scratch_shapes=streams(sz, a.shape[0]),
        compiler_params=params(),
        cost_estimate=cost(sz, a.shape[0]),
        name="rest_fields",
    )(*zs, a, point, tabs["gw"])


def call_final_own(sz, z, fields, point, tabs):
    return pl.pallas_call(
        functools.partial(final_own_kernel, sz),
        in_specs=[VMEM] + [HBM] * len(fields) + [VMEM, HBM],
        out_specs=HBM,
        out_shape=shape_of(sz.micro, sz.flat, sz.cols),
        scratch_shapes=streams(sz, sz.micro),
        compiler_params=params(),
        cost_estimate=cost(sz, sz.own),
        name="final_own",
    )(z, *fields, point, tabs["gw"])


def call_final_rest(sz, steps, zs, out, rest, point, tabs):
    return pl.pallas_call(
        functools.partial(final_rest_kernel, sz, steps),
        in_specs=[VMEM] * len(zs) + [HBM, HBM, VMEM, HBM],
        out_specs=HBM,
        out_shape=shape_of(*out.shape),
        scratch_shapes=streams(sz, max(2, len(zs) * sz.own)),
        input_output_aliases={len(zs): 0},
        compiler_params=params(),
        cost_estimate=cost(sz, len(zs) * sz.own),
        name="final_rest",
    )(*zs, out, rest, point, tabs["gw"])


def call_mix(sz, layer, recv, weights, tabs):
    modes_h = tabs["eh"].shape[1] // 2
    return pl.pallas_call(
        functools.partial(mix_kernel, sz, layer),
        in_specs=[VMEM, VMEM, VMEM] + [HBM] * sz.section,
        out_specs=VMEM,
        out_shape=shape_of(sz.space, sz.section, 2, sz.rows, sz.inv * sz.chans),
        scratch_shapes=[
            pltpu.VMEM((sz.modes, sz.micro, 2, sz.chans, modes_h), F32),
            pltpu.VMEM(weights[0].shape, BF16),
            pltpu.VMEM((sz.micro * sz.modes * sz.chans, 2 * modes_h), BF16),
            pltpu.SemaphoreType.DMA,
        ],
        compiler_params=params(),
        cost_estimate=pl.CostEstimate(flops=4_000_000_000, bytes_accessed=2_000_000, transcendentals=0),
        name="mix",
    )(recv, tabs["eh"], tabs["git"], *weights)


def exchange(value, count):
    return lax.all_to_all(value, BOTH, split_axis=0, concat_axis=0, tiled=True)


def tie(*values):
    return lax.optimization_barrier(values)


def swap(value, step, count, parity=None):
    pairs = [(i, i ^ step) for i in range(count) if parity is None or i % 2 == parity]
    return lax.ppermute(value, "section", pairs)


def on_device(features, lift_w, spec_w, point_w, point_b):
    space = lax.axis_size("space")
    section = lax.axis_size("section")
    pos = lax.axis_index("section")
    micro, feats, rows, cols = features.shape
    chans = lift_w.shape[1]
    local = spec_w.shape[1]
    modes_h = spec_w.shape[2]
    modes_w = local * space
    height = rows * space
    modes = -(-local // section)
    spare = modes * section - local
    sz = Sizes(space, section, rows, chans, micro // section, modes, cols)

    order = mode_order(space, section, local, modes)
    known = (order >= 0)[:, None, :]
    slot = np.stack([2 * order, 2 * order + 1], axis=1) * known
    fw = np.where(known.reshape(1, modes, 1, -1), fwd_w_table(cols, modes_w).astype(np.float32)[:, slot], 0.0)
    gw = np.where(known[..., None], inv_w_table(cols, modes_w).astype(np.float32)[slot], 0.0)
    gw = gw.transpose(1, 0, 2, 3).reshape(sz.slots, cols)
    tabs = {
        "fw": fw.reshape(cols, sz.slots).astype(BF16),
        "gw": (0.5 * gw).astype(BF16),
        "eh": fwd_h_table(height, modes_h),
        "git": np.ascontiguousarray(inv_h_table(height, modes_h).T),
    }
    tabs = {name: jnp.asarray(table) for name, table in tabs.items()}

    point = jnp.concatenate([point_w[0], point_b, jnp.zeros((7, chans), BF16)], axis=0)
    point = jnp.stack([point] + [swap(point, d, section) for d in range(1, section)], axis=0)

    weights = spec_w[0].transpose(0, 2, 3, 1)
    weights = jnp.pad(weights, ((0, spare), (0, 0), (0, 0), (0, 0)))
    weights = weights.reshape((section, modes) + weights.shape[1:])
    parts = {0: lax.dynamic_index_in_dim(weights, pos, 0, keepdims=False)}
    even = []
    for d in range(section - 1, 1, -1):
        parts[d] = lax.dynamic_index_in_dim(weights, pos ^ d, 0, keepdims=False)
        even.insert(0, swap(parts[d], d, section, 0))
        weights, _ = tie(weights, parts[d])
    parts[1] = lax.dynamic_index_in_dim(weights, pos ^ 1, 0, keepdims=False)
    near = swap(parts[1], 1, section)
    early = [parts[0], near] + even

    lift_mat = jnp.einsum("fc,rs->crfs", lift_w, jnp.eye(rows, dtype=BF16)).reshape(sz.flat, feats * rows)
    flat = features.reshape(section, sz.own, feats * rows, cols)
    feat = [lax.dynamic_index_in_dim(flat, pos ^ d, 0, keepdims=False) for d in range(section)]
    field, send = call_lift(sz, feat[0], lift_mat, tabs)
    others = jnp.concatenate(feat[1:], axis=0)

    fields = []
    zs = []
    for layer in range(section):
        recv = exchange(send, sz.devices).reshape(space, section, sz.own, rows, sz.fwd * chans)
        back = call_mix(sz, layer, recv, late if layer % 2 else early, tabs)
        if layer == 0:
            back, others, point, *far = tie(back, others, point, *[parts[d] for d in range(2, section)])
            odd = [swap(far[d - 2], d, section, 1) for d in range(2, section)]
            late = [parts[0], near] + odd
        else:
            back, *zs = tie(back, *zs)
        back = exchange(back.reshape(sz.devices, 2, rows, sz.inv * chans), sz.devices)
        if layer == 0:
            rest = call_lift_rest(sz, others, lift_mat)
        else:
            rest = call_rest(sz, layer - 1, zs, rest, point, tabs)
            fields.append(rest)
        back, rest = tie(back, rest)
        if layer + 1 < section:
            field, z, send = call_own(sz, layer, back, field, point, tabs)
            zs = [swap(z, d, section) for d in range(1, section)]
            fields.append(field)
        else:
            z = call_unpack(sz, back)
            zs = [swap(z, d, section) for d in range(1, section)]
            out = call_final_own(sz, z, fields, point, tabs)
            out = call_final_rest(sz, [1], zs[:1], out, rest, point, tabs)
            if section > 2:
                out = call_final_rest(sz, list(range(2, section)), zs[1:], out, rest, point, tabs)
    return out.reshape(1, micro, chans, rows, cols)


def solution(mesh):
    in_specs = (
        P(None, None, "space", None),
        P(),
        P("section", "space", None, None, None),
        P("section", None, None),
        P("section", None),
    )
    out_specs = P("section", None, None, "space", None)
    return jax.shard_map(on_device, mesh=mesh, in_specs=in_specs, out_specs=out_specs, check_vma=False)
```

```python
import functools

import jax
import jax.numpy as jnp
import numpy as np
from jax import lax
from jax.experimental import pallas as pl
from jax.experimental.pallas import tpu as pltpu
from jax.sharding import PartitionSpec as P

BF16 = jnp.bfloat16
F32 = jnp.float32
BOTH = ("space", "section")


def turn_table(first, second, period):
    product = (first[:, None] * second[None, :]) % period
    return (np.float32(2.0 * np.pi) * product.astype(np.float32) / np.float32(period)).astype(np.float32)


def row_freqs(height, modes_h):
    index = np.arange(modes_h)
    return np.where(index < modes_h // 2, index, height - modes_h + index)


def mode_order(space, section, local, modes):
    part = np.arange(section)[None, None, :] * modes + np.arange(modes)[:, None, None]
    whole = np.arange(space)[None, :, None] * local + part
    return np.where(part < local, whole, -1).reshape(modes, space * section)


def fwd_w_table(cols, modes_w):
    slot = np.arange(2 * modes_w)
    angle = turn_table(np.arange(cols), slot // 2, cols)
    return np.where(slot[None, :] % 2 == 0, np.cos(angle), -np.sin(angle)).astype(BF16)


def fwd_h_table(height, modes_h):
    angle = turn_table(np.arange(height), row_freqs(height, modes_h), height)
    return np.concatenate([np.cos(angle), np.sin(angle)], axis=1).astype(BF16)


def inv_h_table(height, modes_h):
    angle = turn_table(row_freqs(height, modes_h), np.arange(height), height)
    cosine = np.cos(angle) / height
    sine = np.sin(angle) / height
    upper = np.concatenate([cosine, sine], axis=1)
    lower = np.concatenate([-sine, cosine], axis=1)
    return np.concatenate([upper, lower], axis=0).astype(BF16)


def inv_w_table(cols, modes_w):
    slot = np.arange(2 * modes_w)
    mode = slot // 2
    angle = turn_table(mode, np.arange(cols), cols)
    factor = np.where(mode == 0, 1.0, 2.0).astype(np.float32)[:, None] / cols
    return np.where(slot[:, None] % 2 == 0, factor * np.cos(angle), -factor * np.sin(angle)).astype(BF16)


def gelu(half):
    half = half.astype(BF16)
    inner = half * (BF16(1.5957691216057308) + BF16(0.2854192650890401) * (half * half))
    return half + half * jnp.tanh(inner)


def dot(left, right):
    return jnp.dot(left, right, preferred_element_type=F32)


def dot_tn(left, right):
    return lax.dot_general(left, right, (((0,), (0,)), ((), ())), preferred_element_type=F32)


def dot_nt(left, right):
    return lax.dot_general(left, right, (((1,), (1,)), ((), ())), preferred_element_type=F32)


class Sizes:
    def __init__(self, space, section, rows, chans, own, modes, cols):
        self.space, self.section, self.rows, self.chans = space, section, rows, chans
        self.own, self.modes, self.cols = own, modes, cols
        self.devices = space * section
        self.micro = own * section
        self.flat = chans * rows
        self.chunk = min(rows, max(1, 128 // chans))
        self.turns = rows // self.chunk
        self.fwd = 2 * modes
        self.inv = own * modes
        self.slots = 2 * modes * self.devices
        self.note = -(-(chans + 1) // 16) * 16
        self.step = min(512, cols)
        self.parts = cols // self.step


def iota(shape, axis):
    return lax.broadcasted_iota(jnp.int32, shape, axis)


def build_swap(ref, left, right, inner):
    size = left * right * inner
    row = iota((size, 1), 0)
    first, second, third = row // (right * inner), row // inner % right, row % inner
    target = (second * left + first) * inner + third
    ref[...] = jnp.where(iota((size, size), 1) == target, 1.0, 0.0).astype(BF16)


def build_mat(sz, layer, point_ref, mat_ref, bias_ref):
    pos = lax.axis_index("section")
    start = point_ref.shape[1] - sz.note
    block = point_ref[pos ^ layer, start:, : sz.chans] * BF16(0.5)
    expand = jnp.where(iota((sz.flat, sz.chans), 0) // sz.rows == iota((sz.flat, sz.chans), 1), 1.0, 0.0).astype(BF16)
    spread = dot_nt(expand, block[: sz.chans]).astype(BF16)
    full = dot_nt(spread, expand)
    same = iota((sz.flat, 1), 0) % sz.rows == iota((1, sz.flat), 1) % sz.rows
    mat_ref[...] = jnp.where(same, full, 0.0).astype(BF16)
    bias = jnp.broadcast_to(block[sz.chans : sz.chans + 1], (128, sz.chans))
    bias = jnp.where(iota(bias.shape, 0) == 0, bias.astype(F32), 0.0).astype(BF16)
    bias_ref[...] = dot_nt(expand, bias).astype(BF16)


def one_field(sz, z_ref, a_ref, mat_ref, bias_ref, gw_ref, out_ref, load, store):
    left = jnp.concatenate([mat_ref[...], z_ref[...], bias_ref[...]], axis=1)
    ones = jnp.ones((128, sz.step), BF16)
    for part in range(sz.cols // sz.step):
        cols = slice(part * sz.step, (part + 1) * sz.step)
        if part < len(load):
            load[part].wait()
        right = jnp.concatenate([a_ref[:, cols], gw_ref[:, cols], ones], axis=0)
        out_ref[:, cols] = gelu(dot(left, right))
        if len(store) == sz.parts or part == sz.parts - 1:
            store[min(part, len(store) - 1)].start()


def pack(sz, at, field_ref, fw_ref, order_ref, swap_ref, stage_ref, send_ref):
    count, wide = sz.devices, sz.chunk * sz.chans
    spectrum = dot(field_ref[...], fw_ref[...]).astype(BF16)
    turned = dot_tn(spectrum, order_ref[...]).astype(BF16)
    parts = []
    for t in range(sz.turns):
        lanes = slice(t * wide, (t + 1) * wide)
        parts.append(jnp.concatenate([turned[k * count : (k + 1) * count, lanes] for k in range(sz.fwd)], axis=1))
    moved = dot(jnp.concatenate(parts, axis=0), swap_ref[...])
    width = sz.fwd * sz.chans
    for t in range(sz.turns):
        for r in range(sz.chunk):
            place = (t * sz.chunk + r) * count
            stage_ref[place : place + count, :] = moved[t * count : (t + 1) * count, r * width : (r + 1) * width]
    for device in range(count):
        send_ref[device, at] = stage_ref[pl.ds(device, sz.rows, stride=count), :].astype(BF16)


def unpack(sz, back_ref, order_ref, swap_ref, stage_ref, turned_ref, z_ref):
    count, wide = sz.devices, sz.chunk * sz.chans
    width = sz.inv * sz.chans
    for q in range(2):
        for device in range(count):
            stage_ref[pl.ds(device, sz.rows, stride=count), :] = back_ref[device, q].astype(F32)
        parts = []
        for t in range(sz.turns):
            blocks = [
                stage_ref[(t * sz.chunk + r) * count : (t * sz.chunk + r + 1) * count, :] for r in range(sz.chunk)
            ]
            parts.append(jnp.concatenate(blocks, axis=1))
        moved = dot(jnp.concatenate(parts, axis=0).astype(BF16), swap_ref[...]).astype(BF16)
        for t in range(sz.turns):
            for k in range(sz.inv):
                m, mode = divmod(k, sz.modes)
                place = (q * sz.modes + mode) * count
                turned_ref[m, place : place + count, t * wide : (t + 1) * wide] = moved[
                    t * count : (t + 1) * count, k * wide : (k + 1) * wide
                ]
    for m in range(sz.own):
        z_ref[m] = dot_nt(order_ref[...], turned_ref[m]).astype(BF16)


def copy_in(source, target, sem):
    copy = pltpu.make_async_copy(source, target, sem)
    copy.start()
    return copy


def copies(sz, source, target, sem, slot, cut):
    if not cut:
        return [pltpu.make_async_copy(source, target, sem.at[slot, 0])]
    made = []
    for part in range(sz.parts):
        cols = pl.ds(part * sz.step, sz.step)
        made.append(pltpu.make_async_copy(source.at[:, cols], target.at[:, cols], sem.at[slot, part]))
    return made


def lift_kernel(sz, feat_ref, mat_ref, out_ref, held_ref, out_sem):
    stores = []
    for i in range(feat_ref.shape[0]):
        if i >= 2:
            stores[i - 2].wait()
        held_ref[i % 2] = dot(mat_ref[...], feat_ref[i]).astype(BF16)
        stores.append(copy_in(held_ref.at[i % 2], out_ref.at[i], out_sem.at[i % 2]))
    for store in stores[-2:]:
        store.wait()


def own_kernel(sz, layer, back_ref, a_hbm, point_ref, gw_hbm, fw_hbm, out_ref, z_ref, send_ref, *scratch):
    (mat_ref, bias_ref, in_ref, held_ref, in_sem, out_sem, gw_ref, tab_sem,
     fw_ref, order_ref, swap_f_ref, swap_i_ref, stage_f_ref, stage_i_ref, turned_ref) = scratch
    gw_load = copy_in(gw_hbm, gw_ref, tab_sem.at[0])
    loads = [copies(sz, a_hbm.at[m], in_ref.at[m], in_sem, m, m == 0) for m in range(sz.own)]
    for copy in sum(loads, []):
        copy.start()
    fw_load = copy_in(fw_hbm, fw_ref, tab_sem.at[1])
    build_swap(order_ref, sz.chans, sz.rows, 1)
    build_swap(swap_i_ref, sz.chunk, sz.inv, sz.chans)
    build_swap(swap_f_ref, sz.fwd, sz.chunk, sz.chans)
    build_mat(sz, layer, point_ref, mat_ref, bias_ref)
    unpack(sz, back_ref, order_ref, swap_i_ref, stage_i_ref, turned_ref, z_ref)
    gw_load.wait()
    stores = []
    for m in range(sz.own):
        store = copies(sz, held_ref.at[m], out_ref.at[m], out_sem, m, False)
        one_field(sz, z_ref.at[m], in_ref.at[m], mat_ref, bias_ref, gw_ref, held_ref.at[m], loads[m], store)
        stores += store
        if m == 0:
            fw_load.wait()
        pack(sz, m, held_ref.at[m], fw_ref, order_ref, swap_f_ref, stage_f_ref, send_ref)
    for store in stores:
        store.wait()


def unpack_kernel(sz, back_ref, z_ref, order_ref, swap_ref, stage_ref, turned_ref):
    build_swap(order_ref, sz.chans, sz.rows, 1)
    build_swap(swap_ref, sz.chunk, sz.inv, sz.chans)
    unpack(sz, back_ref, order_ref, swap_ref, stage_ref, turned_ref, z_ref)


def run_fields(sz, layer, jobs, point_ref, gw_hbm, scratch):
    mat_ref, bias_ref, in_ref, held_ref, in_sem, out_sem, gw_ref, tab_sem = scratch
    gw_load = copy_in(gw_hbm, gw_ref, tab_sem.at[0])
    loads = [copies(sz, job[1], in_ref.at[i], in_sem, i, i == 0) for i, job in enumerate(jobs)]
    for copy in sum(loads, []):
        copy.start()
    build_mat(sz, layer, point_ref, mat_ref, bias_ref)
    gw_load.wait()
    stores = []
    for i, (z_ref, _, target) in enumerate(jobs):
        if i >= 2:
            for store in stores[i - 2]:
                store.wait()
        stores.append(copies(sz, held_ref.at[i % 2], target, out_sem, i % 2, i == len(jobs) - 1))
        one_field(sz, z_ref, in_ref.at[i], mat_ref, bias_ref, gw_ref, held_ref.at[i % 2], loads[i], stores[i])
    for store in sum(stores[-2:], []):
        store.wait()


def run_copies(jobs, scratch):
    _, _, in_ref, _, in_sem, out_sem, _, _ = scratch
    loads = [copy_in(source, in_ref.at[i], in_sem.at[i, 0]) for i, (source, _) in enumerate(jobs)]
    stores = []
    for i, (_, target) in enumerate(jobs):
        loads[i].wait()
        stores.append(copy_in(in_ref.at[i], target, out_sem.at[i, 0]))
    for store in stores:
        store.wait()


def rest_kernel(sz, layer, *refs):
    z_refs = refs[: sz.section - 1]
    a_ref, point_ref, gw_hbm, out_ref = refs[sz.section - 1 : sz.section + 3]
    jobs = []
    for step in range(1, sz.section):
        for m in range(sz.own):
            at = (step - 1) * sz.own + m
            jobs.append((z_refs[step - 1].at[m], a_ref.at[at], out_ref.at[at]))
    run_fields(sz, layer, jobs, point_ref, gw_hbm, refs[sz.section + 3 :])


def final_own_kernel(sz, z_ref, *refs):
    count = sz.section
    fields = refs[: 2 * count - 2]
    point_ref, gw_hbm, out_ref = refs[2 * count - 2 : 2 * count + 1]
    scratch = refs[2 * count + 1 :]
    pos = lax.axis_index("section")
    for layer in range(count - 1):

        @pl.when(pos == layer)
        def _():
            jobs = []
            for step in range(count):
                for m in range(sz.own):
                    place = fields[2 * layer + 1].at[(step - 1) * sz.own + m] if step else fields[2 * layer].at[m]
                    jobs.append((place, out_ref.at[(layer ^ step) * sz.own + m]))
            run_copies(jobs, scratch)

    @pl.when(pos == count - 1)
    def _():
        mine = fields[2 * count - 4]
        jobs = [(z_ref.at[m], mine.at[m], out_ref.at[(count - 1) * sz.own + m]) for m in range(sz.own)]
        run_fields(sz, count - 1, jobs, point_ref, gw_hbm, scratch)


def final_rest_kernel(sz, steps, *refs):
    z_refs = refs[: len(steps)]
    _, rest_ref, point_ref, gw_hbm, out_ref = refs[len(steps) : len(steps) + 5]
    last = sz.section - 1

    @pl.when(lax.axis_index("section") == last)
    def _():
        jobs = []
        for z_ref, step in zip(z_refs, steps):
            for m in range(sz.own):
                target = out_ref.at[(last ^ step) * sz.own + m]
                jobs.append((z_ref.at[m], rest_ref.at[(step - 1) * sz.own + m], target))
        run_fields(sz, last, jobs, point_ref, gw_hbm, refs[len(steps) + 5 :])


def split_kernel(sz, feats, source_ref, lift_ref, note_ref, *refs):
    count = sz.section
    part_refs = refs[: count - 1] + (refs[-2],)
    out_refs = refs[count - 1 : 2 * count - 1]
    sem = refs[-1]
    pos = lax.axis_index("section")
    made = [copy_in(source_ref.at[pos ^ (d + 1) if d < count - 1 else pos], part_refs[d], sem.at[d]) for d in range(count)]
    for d in range(count):
        part_ref, out_ref = part_refs[d], out_refs[(d + 1) % count]
        made[d].wait()
        for mode in range(sz.modes):

            def body(c, accs):
                weight = part_ref[mode, c].astype(F32)
                return tuple(acc + lift_ref[f, c] * weight for f, acc in enumerate(accs))

            zero = jnp.zeros(part_ref.shape[2:], F32)
            sums = lax.fori_loop(0, sz.chans, body, (zero,) * feats, unroll=4)
            for f in range(feats):
                size = zero.shape[0]
                at = (mode * feats + f) * size
                out_ref[at : at + size] = sums[f].astype(BF16)
        out_ref[out_ref.shape[0] - sz.note :] = note_ref[...]


def pick_kernel(sz, layer, source_ref, *refs):
    parts, (_, out_ref, sem) = refs[:-3], refs[-3:]
    pos = lax.axis_index("section")
    for step in range(sz.section):

        @pl.when(pos == (layer ^ step))
        def _():
            source = parts[step - 1] if step else source_ref.at[layer]
            copy_in(source, out_ref, sem).wait()


def send_back(sz, git_ref, y_ref, out_ref):
    back = dot_nt(git_ref[...], y_ref[...]).astype(BF16)
    lanes = sz.inv * sz.chans
    height = sz.space * sz.rows
    for sp in range(sz.space):
        for dest in range(sz.section):
            for q in range(2):
                start = q * height + sp * sz.rows
                out_ref[sp, dest, q] = back[start : start + sz.rows, dest * lanes : (dest + 1) * lanes]


def first_mix_kernel(sz, feats, cols_ref, folded_ref, eh_ref, git_ref, out_ref, p_ref, y_ref):
    chans = sz.chans
    modes_h = eh_ref.shape[1] // 2
    folded = folded_ref.at[lax.axis_index("section")]
    p_ref[...] = dot(cols_ref[...], eh_ref[...])
    for mode in range(sz.modes):
        for m in range(sz.micro):
            out_re = jnp.zeros((chans, modes_h), F32)
            out_im = jnp.zeros((chans, modes_h), F32)
            for f in range(feats):
                at = (m * sz.modes + mode) * 2 * feats + f
                real, imag = p_ref[at : at + 1, :], p_ref[at + feats : at + feats + 1, :]
                x_re = real[:, :modes_h] + imag[:, modes_h:]
                x_im = imag[:, :modes_h] - real[:, modes_h:]
                at = (mode * feats + f) * 2 * chans
                w_re = folded[at : at + chans, :].astype(F32)
                w_im = folded[at + chans : at + 2 * chans, :].astype(F32)
                out_re += x_re * w_re - x_im * w_im
                out_im += x_re * w_im + x_im * w_re
            at = (m * sz.modes + mode) * chans
            y_ref[at : at + chans, :modes_h] = out_re.astype(BF16)
            y_ref[at : at + chans, modes_h:] = out_im.astype(BF16)
    send_back(sz, git_ref, y_ref, out_ref)


def mix_kernel(sz, recv_ref, w_ref, eh_ref, git_hbm, out_ref, x_ref, y_ref, git_ref, sem):
    load = copy_in(git_hbm, git_ref, sem)
    modes_h = eh_ref.shape[1] // 2
    chans = sz.chans
    for src in range(sz.section):
        for m in range(sz.own):
            cols = recv_ref[:, src, m].reshape(sz.space * sz.rows, sz.fwd * chans)
            proj = dot_tn(cols, eh_ref[...])
            for mode in range(sz.modes):
                real = proj[2 * mode * chans : (2 * mode + 1) * chans]
                imag = proj[(2 * mode + 1) * chans : (2 * mode + 2) * chans]
                x_ref[mode, src * sz.own + m, 0] = real[:, :modes_h] + imag[:, modes_h:]
                x_ref[mode, src * sz.own + m, 1] = imag[:, :modes_h] - real[:, modes_h:]
    group = min(4, sz.micro)
    for mode in range(sz.modes):
        for base in range(0, sz.micro, group):

            def body(c, accs):
                weight = w_ref[mode, c].astype(F32)
                w_re = weight[:chans]
                w_im = weight[chans:]
                new = []
                for g in range(group):
                    x_re = x_ref[mode, base + g, 0, pl.ds(c, 1), :]
                    x_im = x_ref[mode, base + g, 1, pl.ds(c, 1), :]
                    re, im = accs[2 * g], accs[2 * g + 1]
                    new.append(re + (x_re * w_re - x_im * w_im))
                    new.append(im + (x_re * w_im + x_im * w_re))
                return tuple(new)

            zero = jnp.zeros((chans, modes_h), F32)
            accs = lax.fori_loop(0, chans, body, (zero,) * (2 * group), unroll=4)
            for g in range(group):
                at = ((base + g) * sz.modes + mode) * chans
                y_ref[at : at + chans, :modes_h] = accs[2 * g].astype(BF16)
                y_ref[at : at + chans, modes_h:] = accs[2 * g + 1].astype(BF16)
    load.wait()
    send_back(sz, git_ref, y_ref, out_ref)


HBM = pl.BlockSpec(memory_space=pltpu.HBM)
VMEM = pl.BlockSpec(memory_space=pltpu.VMEM)


def params(size=52):
    return pltpu.CompilerParams(vmem_limit_bytes=size * 1024 * 1024)


def cost(sz, fields, extra=0):
    return pl.CostEstimate(
        flops=fields * 2 * sz.flat * sz.cols * (sz.flat + 256) + extra,
        bytes_accessed=fields * 4 * sz.flat * sz.cols,
        transcendentals=fields * sz.flat * sz.cols,
    )


def shape_of(*shape, dtype=BF16):
    return jax.ShapeDtypeStruct(shape, dtype)


def stage_f(sz):
    return pltpu.VMEM((sz.rows * sz.devices, sz.fwd * sz.chans), F32)


def stage_i(sz):
    return pltpu.VMEM((sz.rows * sz.devices, sz.inv * sz.chans), F32)


def turned(sz):
    return pltpu.VMEM((sz.own, sz.slots, sz.flat), BF16)


def send_shape(sz):
    return shape_of(sz.devices, sz.own, sz.rows, sz.fwd * sz.chans)


def square(*sizes):
    size = int(np.prod(sizes))
    return pltpu.VMEM((size, size), BF16)


def sems(*counts):
    return pltpu.SemaphoreType.DMA(counts)


def streams(sz, jobs):
    return [
        square(sz.flat),
        pltpu.VMEM((sz.flat, 128), BF16),
        pltpu.VMEM((jobs, sz.flat, sz.cols), BF16),
        pltpu.VMEM((2, sz.flat, sz.cols), BF16),
        sems(jobs, sz.parts),
        sems(jobs, sz.parts),
        pltpu.VMEM((sz.slots, sz.cols), BF16),
        sems(2),
    ]


def call_lift(sz, feat, mat):
    return pl.pallas_call(
        functools.partial(lift_kernel, sz),
        in_specs=[VMEM, VMEM],
        out_specs=HBM,
        out_shape=shape_of(feat.shape[0], sz.flat, sz.cols),
        scratch_shapes=[pltpu.VMEM((2, sz.flat, sz.cols), BF16), sems(2)],
        compiler_params=params(),
        cost_estimate=cost(sz, feat.shape[0]),
        name="lift",
    )(feat, mat)


def call_own(sz, layer, back, a, point, tabs):
    return pl.pallas_call(
        functools.partial(own_kernel, sz, layer),
        in_specs=[VMEM, HBM, VMEM, HBM, HBM],
        out_specs=[HBM, VMEM, VMEM],
        out_shape=[shape_of(*a.shape), shape_of(sz.own, sz.flat, sz.slots), send_shape(sz)],
        scratch_shapes=streams(sz, max(sz.own, 2))
        + [
            pltpu.VMEM((sz.cols, sz.slots), BF16),
            square(sz.flat),
            square(sz.fwd, sz.chunk, sz.chans),
            square(sz.inv, sz.chunk, sz.chans),
            stage_f(sz),
            stage_i(sz),
            turned(sz),
        ],
        compiler_params=params(),
        cost_estimate=cost(sz, sz.own),
        name="own_field",
    )(back, a, point, tabs["gw"], tabs["fw"])


def call_unpack(sz, back):
    return pl.pallas_call(
        functools.partial(unpack_kernel, sz),
        in_specs=[VMEM],
        out_specs=VMEM,
        out_shape=shape_of(sz.own, sz.flat, sz.slots),
        scratch_shapes=[square(sz.flat), square(sz.inv, sz.chunk, sz.chans), stage_i(sz), turned(sz)],
        compiler_params=params(),
        cost_estimate=cost(sz, 1),
        name="unpack",
    )(back)


def call_rest(sz, layer, zs, a, point, tabs):
    return pl.pallas_call(
        functools.partial(rest_kernel, sz, layer),
        in_specs=[VMEM] * len(zs) + [HBM, VMEM, HBM],
        out_specs=HBM,
        out_shape=shape_of(*a.shape),
        scratch_shapes=streams(sz, a.shape[0]),
        compiler_params=params(),
        cost_estimate=cost(sz, a.shape[0]),
        name="rest_fields",
    )(*zs, a, point, tabs["gw"])


def call_final_own(sz, z, fields, point, tabs):
    return pl.pallas_call(
        functools.partial(final_own_kernel, sz),
        in_specs=[VMEM] + [HBM] * len(fields) + [VMEM, HBM],
        out_specs=HBM,
        out_shape=shape_of(sz.micro, sz.flat, sz.cols),
        scratch_shapes=streams(sz, sz.micro),
        compiler_params=params(),
        cost_estimate=cost(sz, sz.own),
        name="final_own",
    )(z, *fields, point, tabs["gw"])


def call_final_rest(sz, steps, zs, out, rest, point, tabs):
    return pl.pallas_call(
        functools.partial(final_rest_kernel, sz, steps),
        in_specs=[VMEM] * len(zs) + [HBM, HBM, VMEM, HBM],
        out_specs=HBM,
        out_shape=shape_of(*out.shape),
        scratch_shapes=streams(sz, max(2, len(zs) * sz.own)),
        input_output_aliases={len(zs): 0},
        compiler_params=params(),
        cost_estimate=cost(sz, len(zs) * sz.own),
        name="final_rest",
    )(*zs, out, rest, point, tabs["gw"])


def call_split(sz, feats, weights, lift, note):
    part = weights.shape[1:]
    message = shape_of(sz.modes * feats * part[2] + sz.note, part[3])
    smem = pl.BlockSpec(memory_space=pltpu.SMEM)
    outs = [shape_of(*part)] * (sz.section - 1) + [message] * sz.section
    made = pl.pallas_call(
        functools.partial(split_kernel, sz, feats),
        in_specs=[HBM, smem, VMEM],
        out_specs=[VMEM] * len(outs),
        out_shape=outs,
        scratch_shapes=[pltpu.VMEM(part, BF16), sems(sz.section)],
        compiler_params=params(),
        name="split",
    )(weights, lift, note)
    return made[: sz.section - 1], made[sz.section - 1 :]


def call_first_mix(sz, feats, cols, messages, tabs):
    modes_h = tabs["eh"].shape[1] // 2
    return pl.pallas_call(
        functools.partial(first_mix_kernel, sz, feats),
        in_specs=[VMEM] * 4,
        out_specs=VMEM,
        out_shape=shape_of(sz.space, sz.section, 2, sz.rows, sz.inv * sz.chans),
        scratch_shapes=[
            pltpu.VMEM((cols.shape[0], 2 * modes_h), F32),
            pltpu.VMEM((sz.micro * sz.modes * sz.chans, 2 * modes_h), BF16),
        ],
        compiler_params=params(),
        name="first_mix",
    )(cols, messages, tabs["eh"], tabs["git"])


def call_pick(sz, layer, weights, parts, after):
    return pl.pallas_call(
        functools.partial(pick_kernel, sz, layer),
        in_specs=[HBM] * (sz.section + 1),
        out_specs=VMEM,
        out_shape=shape_of(*weights.shape[1:]),
        scratch_shapes=[pltpu.SemaphoreType.DMA],
        compiler_params=params(),
        name="pick",
    )(weights, *parts, after)


def call_mix(sz, recv, weights, tabs):
    modes_h = tabs["eh"].shape[1] // 2
    return pl.pallas_call(
        functools.partial(mix_kernel, sz),
        in_specs=[VMEM, VMEM, VMEM, HBM],
        out_specs=VMEM,
        out_shape=shape_of(sz.space, sz.section, 2, sz.rows, sz.inv * sz.chans),
        scratch_shapes=[
            pltpu.VMEM((sz.modes, sz.micro, 2, sz.chans, modes_h), F32),
            pltpu.VMEM((sz.micro * sz.modes * sz.chans, 2 * modes_h), BF16),
            pltpu.VMEM(tabs["git"].shape, BF16),
            pltpu.SemaphoreType.DMA,
        ],
        compiler_params=params(),
        cost_estimate=pl.CostEstimate(flops=4_000_000_000, bytes_accessed=2_000_000, transcendentals=0),
        name="mix",
    )(recv, weights, tabs["eh"], tabs["git"])


def exchange(value, count):
    return lax.all_to_all(value, BOTH, split_axis=0, concat_axis=0, tiled=True)


def tie(*values):
    return lax.optimization_barrier(values)


def swap(value, step, count, sources=None):
    pairs = [(i, i ^ step) for i in range(count) if sources is None or sources(i)]
    return lax.ppermute(value, "section", pairs)


def gather_last(value, count):
    last = count - 1
    return [lax.ppermute(value, "section", [(last ^ step, last)]) for step in range(1, count)]


def on_device(features, lift_w, spec_w, point_w, point_b):
    space = lax.axis_size("space")
    section = lax.axis_size("section")
    pos = lax.axis_index("section")
    micro, feats, rows, cols = features.shape
    chans = lift_w.shape[1]
    local = spec_w.shape[1]
    modes_h = spec_w.shape[2]
    modes_w = local * space
    height = rows * space
    modes = -(-local // section)
    spare = modes * section - local
    sz = Sizes(space, section, rows, chans, micro // section, modes, cols)

    order = mode_order(space, section, local, modes)
    known = (order >= 0)[:, None, :]
    slot = np.stack([2 * order, 2 * order + 1], axis=1) * known
    fw = np.where(known.reshape(1, modes, 1, -1), fwd_w_table(cols, modes_w).astype(np.float32)[:, slot], 0.0)
    gw = np.where(known[..., None], inv_w_table(cols, modes_w).astype(np.float32)[slot], 0.0)
    gw = gw.transpose(1, 0, 2, 3).reshape(sz.slots, cols)
    tabs = {
        "fw": fw.reshape(cols, sz.slots).astype(BF16),
        "gw": (0.5 * gw).astype(BF16),
        "eh": fwd_h_table(height, modes_h),
        "git": np.ascontiguousarray(inv_h_table(height, modes_h).T),
    }
    tabs = {name: jnp.asarray(table) for name, table in tabs.items()}

    weights = spec_w[0].transpose(0, 2, 3, 1)
    weights = jnp.pad(weights, ((0, spare), (0, 0), (0, 0), (0, 0)))
    weights = weights.reshape((section, modes) + weights.shape[1:])
    note = jnp.concatenate([point_w[0], point_b], axis=0)
    note = jnp.pad(note, ((0, sz.note - chans - 1), (0, modes_h - chans)))
    parts, messages = call_split(sz, feats, weights, lift_w.astype(F32), note)
    messages = [messages[0]] + [swap(messages[d], d, section) for d in range(1, section)]

    flat = features.reshape(section, sz.own, feats * rows, cols)
    feat = [lax.dynamic_index_in_dim(flat, pos ^ d, 0, keepdims=False) for d in range(section)]
    send = jnp.einsum("mfrw,wk->kmfr", feat[0].reshape(sz.own, feats, rows, cols), tabs["fw"], preferred_element_type=F32)
    send = send.astype(BF16).reshape(sz.fwd, sz.devices, sz.own * feats * rows).transpose(1, 0, 2)
    recv = exchange(send, sz.devices).reshape(space, section, modes, 2, sz.own, feats, rows)
    recv = recv.transpose(1, 4, 2, 3, 5, 0, 6).reshape(micro * modes * 2 * feats, height)

    point = jnp.stack(messages, axis=0)
    lift_mat = jnp.einsum("fc,rs->crfs", lift_w, jnp.eye(rows, dtype=BF16)).reshape(sz.flat, feats * rows)
    others = jnp.concatenate(feat[1:], axis=0)

    fields = []
    zs = []
    for layer in range(section):
        if layer == 0:
            back = call_first_mix(sz, feats, recv, point, tabs)
            back, mine, others, *parts = tie(back, feat[0], others, *parts)
            near = swap(parts[0], 1, section, lambda i: i > 0)
            held = [near] + [swap(parts[d - 1], d, section, lambda i: 0 < i < section - 1) for d in range(2, section)]
        else:
            if layer == section - 1:
                held = last
            recv = exchange(send, sz.devices).reshape(space, section, sz.own, rows, sz.fwd * chans)
            back = call_mix(sz, recv, call_pick(sz, layer, weights, held, send), tabs)
            back, rest, *zs = tie(back, rest, *zs)
            zs += [swap(zs[steps.index(d - 1)], 1, section) for d in range(3, section, 2)]
            zs = [zs[z_at] for z_at in z_order]
        back = exchange(back.reshape(sz.devices, 2, rows, sz.inv * chans), sz.devices)
        if layer == 0:
            field = call_lift(sz, mine, lift_mat)
            rest = call_lift(sz, others, lift_mat)
        else:
            rest = call_rest(sz, layer - 1, zs, rest, point, tabs)
            fields.append(rest)
        back, rest = tie(back, rest)
        if layer + 1 < section:
            field, z, send = call_own(sz, layer, back, field, point, tabs)
            steps = [1] + list(range(2, section, 2))
            zs = [swap(z, d, section) for d in steps]
            steps += range(3, section, 2)
            z_order = [steps.index(d) for d in range(1, section)]
            fields.append(field)
            if layer == 0:
                send, *far = tie(send, *parts[1:])
                last = [near] + [swap(far[d - 2], d, section, lambda i: i == section - 1) for d in range(2, section)]
        else:
            z = call_unpack(sz, back)
            zs = gather_last(z, section)
            out = call_final_own(sz, z, fields, point, tabs)
            out = call_final_rest(sz, list(range(1, section)), zs, out, rest, point, tabs)
    return out.reshape(1, micro, chans, rows, cols)


def solution(mesh):
    in_specs = (
        P(None, None, "space", None),
        P(),
        P("section", "space", None, None, None),
        P("section", None, None),
        P("section", None),
    )
    out_specs = P("section", None, None, "space", None)
    return jax.shard_map(on_device, mesh=mesh, in_specs=in_specs, out_specs=out_specs, check_vma=False)
```

```python
import functools

import jax
import jax.numpy as jnp
import numpy as np
from jax import lax
from jax.experimental import pallas as pl
from jax.experimental.pallas import tpu as pltpu
from jax.sharding import PartitionSpec as P

BF16 = jnp.bfloat16
F32 = jnp.float32
BOTH = ("space", "section")


def turn_table(first, second, period):
    product = (first[:, None] * second[None, :]) % period
    return (np.float32(2.0 * np.pi) * product.astype(np.float32) / np.float32(period)).astype(np.float32)


def row_freqs(height, modes_h):
    index = np.arange(modes_h)
    return np.where(index < modes_h // 2, index, height - modes_h + index)


def mode_order(space, section, local, modes):
    part = np.arange(section)[None, None, :] * modes + np.arange(modes)[:, None, None]
    whole = np.arange(space)[None, :, None] * local + part
    return np.where(part < local, whole, -1).reshape(modes, space * section)


def fwd_w_table(cols, modes_w):
    slot = np.arange(2 * modes_w)
    angle = turn_table(np.arange(cols), slot // 2, cols)
    return np.where(slot[None, :] % 2 == 0, np.cos(angle), -np.sin(angle)).astype(BF16)


def fwd_h_table(height, modes_h):
    angle = turn_table(np.arange(height), row_freqs(height, modes_h), height)
    return np.concatenate([np.cos(angle), np.sin(angle)], axis=1).astype(BF16)


def inv_h_table(height, modes_h):
    angle = turn_table(row_freqs(height, modes_h), np.arange(height), height)
    cosine = np.cos(angle) / height
    sine = np.sin(angle) / height
    upper = np.concatenate([cosine, sine], axis=1)
    lower = np.concatenate([-sine, cosine], axis=1)
    return np.concatenate([upper, lower], axis=0).astype(BF16)


def inv_w_table(cols, modes_w):
    slot = np.arange(2 * modes_w)
    mode = slot // 2
    angle = turn_table(mode, np.arange(cols), cols)
    factor = np.where(mode == 0, 1.0, 2.0).astype(np.float32)[:, None] / cols
    return np.where(slot[:, None] % 2 == 0, factor * np.cos(angle), -factor * np.sin(angle)).astype(BF16)


def gelu(half):
    half = half.astype(BF16)
    inner = half * (BF16(1.5957691216057308) + BF16(0.2854192650890401) * (half * half))
    return half + half * jnp.tanh(inner)


def dot(left, right):
    return jnp.dot(left, right, preferred_element_type=F32)


def dot_tn(left, right):
    return lax.dot_general(left, right, (((0,), (0,)), ((), ())), preferred_element_type=F32)


def dot_nt(left, right):
    return lax.dot_general(left, right, (((1,), (1,)), ((), ())), preferred_element_type=F32)


class Sizes:
    def __init__(self, space, section, rows, chans, own, modes, cols):
        self.space, self.section, self.rows, self.chans = space, section, rows, chans
        self.own, self.modes, self.cols = own, modes, cols
        self.devices = space * section
        self.micro = own * section
        self.flat = chans * rows
        self.chunk = min(rows, max(1, 128 // chans))
        self.turns = rows // self.chunk
        self.fwd = 2 * modes
        self.inv = own * modes
        self.slots = 2 * modes * self.devices
        self.note = -(-(chans + 1) // 16) * 16
        others = [(step, m) for step in range(1, section) for m in range(own)]
        half = (len(others) + 1) // 3
        self.halves = [others[:half], others[half:]]
        self.step = min(512, cols)
        self.parts = cols // self.step


def iota(shape, axis):
    return lax.broadcasted_iota(jnp.int32, shape, axis)


def build_swap(ref, left, right, inner):
    size = left * right * inner
    row = iota((size, 1), 0)
    first, second, third = row // (right * inner), row // inner % right, row % inner
    target = (second * left + first) * inner + third
    ref[...] = jnp.where(iota((size, size), 1) == target, 1.0, 0.0).astype(BF16)


def build_mat(sz, layer, point_ref, mat_ref, bias_ref):
    pos = lax.axis_index("section")
    block = point_ref[pos ^ layer][:, : sz.chans] * BF16(0.5)
    expand = jnp.where(iota((sz.flat, sz.chans), 0) // sz.rows == iota((sz.flat, sz.chans), 1), 1.0, 0.0).astype(BF16)
    spread = dot_nt(expand, block[: sz.chans]).astype(BF16)
    full = dot_nt(spread, expand)
    same = iota((sz.flat, 1), 0) % sz.rows == iota((1, sz.flat), 1) % sz.rows
    mat_ref[...] = jnp.where(same, full, 0.0).astype(BF16)
    bias = jnp.broadcast_to(block[sz.chans : sz.chans + 1], (128, sz.chans))
    bias = jnp.where(iota(bias.shape, 0) == 0, bias.astype(F32), 0.0).astype(BF16)
    bias_ref[...] = dot_nt(expand, bias).astype(BF16)


def one_field(sz, z_ref, a_ref, mat_ref, bias_ref, gw_ref, out_ref, load, store):
    left = jnp.concatenate([mat_ref[...], z_ref[...], bias_ref[...]], axis=1)
    ones = jnp.ones((128, sz.step), BF16)
    for part in range(sz.cols // sz.step):
        cols = slice(part * sz.step, (part + 1) * sz.step)
        if part < len(load):
            load[part].wait()
        right = jnp.concatenate([a_ref[:, cols], gw_ref[:, cols], ones], axis=0)
        out_ref[:, cols] = gelu(dot(left, right))
        if store and (len(store) == sz.parts or part == sz.parts - 1):
            store[min(part, len(store) - 1)].start()


def pack(sz, field_ref, fw_ref, order_ref, swap_ref, stage_ref, send_ref):
    count, wide = sz.devices, sz.chunk * sz.chans
    spectra = [dot(field_ref[m], fw_ref[...]).astype(BF16) for m in range(sz.own)]
    turned = dot_tn(jnp.concatenate(spectra, axis=1), order_ref[...]).astype(BF16)
    blocks = []
    for m in range(sz.own):
        for t in range(sz.turns):
            lanes = slice(t * wide, (t + 1) * wide)
            starts = [m * sz.slots + k * count for k in range(sz.fwd)]
            blocks.append(jnp.concatenate([turned[start : start + count, lanes] for start in starts], axis=1))
    moved = dot(jnp.concatenate(blocks, axis=0), swap_ref[...])
    width = sz.fwd * sz.chans
    for i in range(sz.own * sz.turns):
        for r in range(sz.chunk):
            place = (i * sz.chunk + r) * count
            stage_ref[place : place + count, :] = moved[i * count : (i + 1) * count, r * width : (r + 1) * width]
    for m in range(sz.own):
        for device in range(count):
            piece = stage_ref[pl.ds(m * sz.rows * count + device, sz.rows, stride=count), :]
            send_ref[device, m] = piece.astype(BF16)


def unpack(sz, back_ref, order_ref, swap_ref, stage_ref, turned_ref, z_ref):
    count, wide = sz.devices, sz.chunk * sz.chans
    for q in range(2):
        for device in range(count):
            place = pl.ds(q * sz.rows * count + device, sz.rows, stride=count)
            stage_ref[place, :] = back_ref[device, q].astype(F32)
    blocks = []
    for i in range(2 * sz.turns):
        starts = [(i * sz.chunk + r) * count for r in range(sz.chunk)]
        blocks.append(jnp.concatenate([stage_ref[start : start + count, :] for start in starts], axis=1))
    moved = dot(jnp.concatenate(blocks, axis=0).astype(BF16), swap_ref[...]).astype(BF16)
    for q in range(2):
        for t in range(sz.turns):
            rows = slice((q * sz.turns + t) * count, (q * sz.turns + t + 1) * count)
            for k in range(sz.inv):
                m, mode = divmod(k, sz.modes)
                place = m * sz.slots + (q * sz.modes + mode) * count
                turned_ref[place : place + count, t * wide : (t + 1) * wide] = moved[rows, k * wide : (k + 1) * wide]
    spectra = dot_nt(order_ref[...], turned_ref[...]).astype(BF16)
    for m in range(sz.own):
        z_ref[m] = spectra[:, m * sz.slots : (m + 1) * sz.slots]


def copy_in(source, target, sem):
    copy = pltpu.make_async_copy(source, target, sem)
    copy.start()
    return copy


def copies(sz, source, target, sem, slot, cut):
    if not cut:
        return [pltpu.make_async_copy(source, target, sem.at[slot, 0])]
    made = []
    for part in range(sz.parts):
        cols = pl.ds(part * sz.step, sz.step)
        made.append(pltpu.make_async_copy(source.at[:, cols], target.at[:, cols], sem.at[slot, part]))
    return made


def lift_kernel(sz, feat_ref, mat_ref, out_ref, held_ref, out_sem):
    stores = []
    for i in range(feat_ref.shape[0]):
        if i >= 2:
            stores[i - 2].wait()
        held_ref[i % 2] = dot(mat_ref[...], feat_ref[i]).astype(BF16)
        stores.append(copy_in(held_ref.at[i % 2], out_ref.at[i], out_sem.at[i % 2]))
    for store in stores[-2:]:
        store.wait()


def own_kernel(sz, layer, back_ref, a_hbm, point_ref, gw_hbm, fw_hbm, out_ref, z_ref, send_ref, *scratch):
    (mat_ref, bias_ref, in_ref, held_ref, in_sem, out_sem, gw_ref, tab_sem,
     fw_ref, order_ref, swap_f_ref, swap_i_ref, stage_f_ref, stage_i_ref, turned_ref) = scratch
    gw_load = copy_in(gw_hbm, gw_ref, tab_sem.at[0])
    loads = [copies(sz, a_hbm.at[m], in_ref.at[m], in_sem, m, m == 0) for m in range(sz.own)]
    for copy in loads[0]:
        copy.start()
    build_swap(order_ref, sz.chans, sz.rows, 1)
    build_swap(swap_i_ref, sz.chunk, sz.inv, sz.chans)
    build_swap(swap_f_ref, sz.fwd, sz.chunk, sz.chans)
    build_mat(sz, layer, point_ref, mat_ref, bias_ref)
    unpack(sz, back_ref, order_ref, swap_i_ref, stage_i_ref, turned_ref, z_ref)
    for copy in sum(loads[1:], []):
        copy.start()
    fw_load = copy_in(fw_hbm, fw_ref, tab_sem.at[1])
    gw_load.wait()
    stores = []
    for m in range(sz.own):
        store = copies(sz, held_ref.at[m], out_ref.at[m], out_sem, m, False)
        one_field(sz, z_ref.at[m], in_ref.at[m], mat_ref, bias_ref, gw_ref, held_ref.at[m], loads[m], store)
        stores += store
    fw_load.wait()
    pack(sz, held_ref, fw_ref, order_ref, swap_f_ref, stage_f_ref, send_ref)
    for store in stores:
        store.wait()


def unpack_kernel(sz, back_ref, z_ref, order_ref, swap_ref, stage_ref, turned_ref):
    build_swap(order_ref, sz.chans, sz.rows, 1)
    build_swap(swap_ref, sz.chunk, sz.inv, sz.chans)
    unpack(sz, back_ref, order_ref, swap_ref, stage_ref, turned_ref, z_ref)


def run_fields(sz, layer, jobs, point_ref, gw_hbm, scratch, others=()):
    mat_ref, bias_ref, in_ref, held_ref, in_sem, out_sem, gw_ref, tab_sem = scratch
    near = others is None
    gw_load = copy_in(gw_hbm, gw_ref, tab_sem.at[0])
    loads = [[] if near else copies(sz, job[1], in_ref.at[i], in_sem, i, i == 0) for i, job in enumerate(jobs)]
    ahead = 2
    for copy in sum(loads[:ahead], []):
        copy.start()
    build_mat(sz, layer, point_ref, mat_ref, bias_ref)
    gw_load.wait()
    stores = []
    for i, (z_ref, source, target) in enumerate(jobs):
        if 0 < i and i + ahead - 1 < len(jobs):
            for copy in loads[i + ahead - 1]:
                copy.start()
        if i >= 2:
            for store in stores[i - 2]:
                store.wait()
        stores.append(copies(sz, held_ref.at[i % 2], target, out_sem, i % 2, i == len(jobs) - 1))
        field = source if near else in_ref.at[i]
        one_field(sz, z_ref, field, mat_ref, bias_ref, gw_ref, held_ref.at[i % 2], loads[i], stores[i])
        if i + 1 == max(1, len(jobs) - 2):
            for copy in others or ():
                copy.start()
    for store in sum(stores[-2:], []) + list(others or ()):
        store.wait()


def run_copies(jobs, scratch):
    _, _, in_ref, _, in_sem, out_sem, _, _ = scratch
    loads = [copy_in(source, in_ref.at[i], in_sem.at[i, 0]) for i, (source, _) in enumerate(jobs)]
    stores = []
    for i, (_, target) in enumerate(jobs):
        loads[i].wait()
        stores.append(copy_in(in_ref.at[i], target, out_sem.at[i, 0]))
    for store in stores:
        store.wait()


def rest_kernel(sz, layer, groups, *refs):
    count, parts = sz.section - 1, len(groups)
    z_refs, a_refs = refs[:count], refs[count : count + parts]
    point_ref, gw_hbm = refs[count + parts : count + parts + 2]
    out_refs, scratch = refs[count + parts + 2 : count + 2 * parts + 2], refs[count + 2 * parts + 2 :]
    jobs = []
    for places, a_ref, out_ref in zip(groups, a_refs, out_refs):
        for i, (step, m) in enumerate(places):
            jobs.append((z_refs[step - 1].at[m], a_ref.at[i], out_ref.at[i]))
    run_fields(sz, layer, jobs, point_ref, gw_hbm, scratch)


def final_own_kernel(sz, steps, z_ref, *refs):
    count = sz.section
    last = count - 1
    z_refs, refs = dict(zip(steps, refs)), refs[len(steps) :]
    fields = refs[: 3 * last]
    point_ref, gw_hbm, out_ref, near_ref = refs[3 * last : 3 * last + 4]
    scratch, near_sem = refs[3 * last + 4 : -1], refs[-1]
    pos = lax.axis_index("section")
    for layer in range(last):

        @pl.when(pos == layer)
        def _():
            own = [((layer * sz.own + m), fields[3 * layer].at[m]) for m in range(sz.own)]
            for half, places in enumerate(sz.halves):
                for i, (step, m) in enumerate(places):
                    own.append(((layer ^ step) * sz.own + m, fields[3 * layer + 1 + half].at[i]))
            run_copies([(place, out_ref.at[at]) for at, place in own], scratch)

    @pl.when(pos == last)
    def _():
        mine = fields[3 * last - 3]
        jobs = [(z_ref.at[m], mine.at[m], out_ref.at[last * sz.own + m]) for m in range(sz.own)]
        for i, (step, m) in enumerate(sz.halves[0]):
            jobs.append((z_refs[step].at[m], fields[3 * last - 2].at[i], out_ref.at[(last ^ step) * sz.own + m]))
        others = [pltpu.make_async_copy(fields[3 * last - 1], near_ref, near_sem)]
        run_fields(sz, last, jobs, point_ref, gw_hbm, scratch, others)


def final_rest_kernel(sz, steps, *refs):
    last = sz.section - 1
    z_refs, refs = dict(zip(steps, refs)), refs[len(steps) :]
    _, near_ref, point_ref, gw_hbm, out_ref = refs[:5]

    @pl.when(lax.axis_index("section") == last)
    def _():
        jobs = []
        for i, (step, m) in enumerate(sz.halves[1]):
            jobs.append((z_refs[step].at[m], near_ref.at[i], out_ref.at[(last ^ step) * sz.own + m]))
        run_fields(sz, last, jobs, point_ref, gw_hbm, refs[5:], None)


def split_kernel(sz, feats, source_ref, lift_hbm, point_hbm, bias_hbm, *refs):
    count = sz.section
    part_refs = refs[: count - 1] + (refs[-6],)
    out_refs = refs[count - 1 : 2 * count - 1]
    lift_ref, point_ref, bias_ref, spread_ref, sem = refs[-5:]
    pos = lax.axis_index("section")
    small = [(lift_hbm, lift_ref), (point_hbm, point_ref), (bias_hbm, bias_ref)]
    small = [copy_in(source, target, sem.at[count + i]) for i, (source, target) in enumerate(small)]
    made = [copy_in(source_ref.at[pos ^ (d + 1) if d < count - 1 else pos], part_refs[d], sem.at[d]) for d in range(count)]
    for copy in small:
        copy.wait()
    square = (sz.chans, sz.chans)
    for f in range(feats):
        row = jnp.broadcast_to(lift_ref[f : f + 1].astype(F32), square)
        diagonal = jnp.where(iota(square, 0) == iota(square, 1), row, 0.0).astype(BF16)
        spread_ref[f] = dot(diagonal, jnp.ones((sz.chans, spread_ref.shape[2]), BF16))
    empty = jnp.zeros((sz.note - sz.chans - 1, sz.chans), F32)
    note = jnp.concatenate([point_ref[0].astype(F32), bias_ref[...].astype(F32), empty], axis=0).astype(BF16)
    for d in range(count):
        part_ref, out_ref = part_refs[d], out_refs[(d + 1) % count]
        made[d].wait()
        for mode in range(sz.modes):

            def body(c, accs):
                weight = part_ref[mode, c].astype(F32)
                return tuple(acc + spread_ref[f, pl.ds(c, 1), :] * weight for f, acc in enumerate(accs))

            zero = jnp.zeros(part_ref.shape[2:], F32)
            sums = lax.fori_loop(0, sz.chans, body, (zero,) * feats, unroll=4)
            for f in range(feats):
                size = zero.shape[0]
                at = (mode * feats + f) * size
                out_ref[at : at + size] = sums[f].astype(BF16)
        start = out_ref.shape[0] - sz.note
        out_ref[start:] = jnp.zeros((sz.note, out_ref.shape[1]), BF16)
        out_ref[start:, : sz.chans] = note


def cut_kernel(sz, source_ref, _, *refs):
    outs, sem = refs[:-1], refs[-1]
    pos = lax.axis_index("section")
    made = [copy_in(source_ref.at[pos ^ (i + 2)], out, sem.at[i]) for i, out in enumerate(outs)]
    for copy in made:
        copy.wait()


def pick_kernel(sz, layer, source_ref, *refs):
    parts, (_, out_ref, sem) = refs[:-3], refs[-3:]
    pos = lax.axis_index("section")
    for step in range(sz.section):

        @pl.when(pos == (layer ^ step))
        def _():
            source = parts[step - 1] if step else source_ref.at[layer]
            copy_in(source, out_ref, sem).wait()


def send_back(sz, git_ref, y_ref, out_ref):
    back = dot_nt(git_ref[...], y_ref[...]).astype(BF16)
    lanes = sz.inv * sz.chans
    height = sz.space * sz.rows
    for sp in range(sz.space):
        for dest in range(sz.section):
            for q in range(2):
                start = q * height + sp * sz.rows
                out_ref[sp, dest, q] = back[start : start + sz.rows, dest * lanes : (dest + 1) * lanes]


def first_mix_kernel(sz, feats, cols_ref, eh_ref, git_hbm, *refs):
    chans = sz.chans
    modes_h = eh_ref.shape[1] // 2
    messages = refs[: sz.section]
    out_ref, p_ref, y_ref, folded_ref, git_ref, sem = refs[sz.section :]
    load = copy_in(git_hbm, git_ref, sem)
    for step in range(sz.section):

        @pl.when(lax.axis_index("section") == step)
        def _():
            folded_ref[...] = messages[step][: folded_ref.shape[0]].astype(F32)

    p_ref[...] = dot(cols_ref[...], eh_ref[...])
    for mode in range(sz.modes):
        for m in range(sz.micro):
            out_re = jnp.zeros((chans, modes_h), F32)
            out_im = jnp.zeros((chans, modes_h), F32)
            for f in range(feats):
                at = (m * sz.modes + mode) * 2 * feats + f
                real, imag = p_ref[at : at + 1, :], p_ref[at + feats : at + feats + 1, :]
                x_re = real[:, :modes_h] + imag[:, modes_h:]
                x_im = imag[:, :modes_h] - real[:, modes_h:]
                at = (mode * feats + f) * 2 * chans
                w_re = folded_ref[at : at + chans, :]
                w_im = folded_ref[at + chans : at + 2 * chans, :]
                out_re += x_re * w_re - x_im * w_im
                out_im += x_re * w_im + x_im * w_re
            at = (m * sz.modes + mode) * chans
            y_ref[at : at + chans, :modes_h] = out_re.astype(BF16)
            y_ref[at : at + chans, modes_h:] = out_im.astype(BF16)
    load.wait()
    send_back(sz, git_ref, y_ref, out_ref)


def mix_kernel(sz, recv_ref, w_ref, eh_ref, git_hbm, out_ref, x_ref, y_ref, git_ref, sem):
    load = copy_in(git_hbm, git_ref, sem)
    modes_h = eh_ref.shape[1] // 2
    chans = sz.chans
    for src in range(sz.section):
        for m in range(sz.own):
            cols = recv_ref[:, src, m].reshape(sz.space * sz.rows, sz.fwd * chans)
            proj = dot_tn(cols, eh_ref[...])
            for mode in range(sz.modes):
                real = proj[2 * mode * chans : (2 * mode + 1) * chans]
                imag = proj[(2 * mode + 1) * chans : (2 * mode + 2) * chans]
                x_re = real[:, :modes_h] + imag[:, modes_h:]
                x_im = imag[:, :modes_h] - real[:, modes_h:]
                x_ref[mode, src * sz.own + m, 0] = x_re
                x_ref[mode, src * sz.own + m, 1] = x_im
                x_ref[mode, src * sz.own + m, 2] = x_re + x_im
    group = min(4, sz.micro)
    piece = 16 if chans % 16 == 0 else chans
    for mode in range(sz.modes):
        for base in range(0, sz.micro, group):
            for first in range(0, chans, piece):

                def body(c, accs):
                    w_re = w_ref[mode, c, first : first + piece].astype(F32)
                    w_im = w_ref[mode, c, chans + first : chans + first + piece].astype(F32)
                    less, more = w_im - w_re, w_im + w_re
                    new = []
                    for g in range(group):
                        x_re, x_im, x_sum = (x_ref[mode, base + g, part, pl.ds(c, 1), :] for part in range(3))
                        both, second, third = accs[3 * g : 3 * g + 3]
                        new += [both + x_sum * w_re, second + x_re * less, third + x_im * more]
                    return tuple(new)

                zero = jnp.zeros((piece, modes_h), F32)
                accs = lax.fori_loop(0, chans, body, (zero,) * (3 * group), unroll=8)
                for g in range(group):
                    both, second, third = accs[3 * g : 3 * g + 3]
                    at = ((base + g) * sz.modes + mode) * chans + first
                    y_ref[at : at + piece, :modes_h] = (both - third).astype(BF16)
                    y_ref[at : at + piece, modes_h:] = (both + second).astype(BF16)
    load.wait()
    send_back(sz, git_ref, y_ref, out_ref)


HBM = pl.BlockSpec(memory_space=pltpu.HBM)
VMEM = pl.BlockSpec(memory_space=pltpu.VMEM)


def params(size=30):
    return pltpu.CompilerParams(vmem_limit_bytes=size * 1024 * 1024)


def cost(sz, fields, extra=0):
    return pl.CostEstimate(
        flops=fields * 2 * sz.flat * sz.cols * (sz.flat + 256) + extra,
        bytes_accessed=fields * 4 * sz.flat * sz.cols,
        transcendentals=fields * sz.flat * sz.cols,
    )


def shape_of(*shape, dtype=BF16):
    return jax.ShapeDtypeStruct(shape, dtype)


def stage_f(sz):
    return pltpu.VMEM((sz.own * sz.rows * sz.devices, sz.fwd * sz.chans), F32)


def stage_i(sz):
    return pltpu.VMEM((2 * sz.rows * sz.devices, sz.inv * sz.chans), F32)


def turned(sz):
    return pltpu.VMEM((sz.own * sz.slots, sz.flat), BF16)


def send_shape(sz):
    return shape_of(sz.devices, sz.own, sz.rows, sz.fwd * sz.chans)


def square(*sizes):
    size = int(np.prod(sizes))
    return pltpu.VMEM((size, size), BF16)


def sems(*counts):
    return pltpu.SemaphoreType.DMA(counts)


def streams(sz, jobs):
    return [
        square(sz.flat),
        pltpu.VMEM((sz.flat, 128), BF16),
        pltpu.VMEM((jobs, sz.flat, sz.cols), BF16),
        pltpu.VMEM((2, sz.flat, sz.cols), BF16),
        sems(jobs, sz.parts),
        sems(jobs, sz.parts),
        pltpu.VMEM((sz.slots, sz.cols), BF16),
        sems(2),
    ]


def placed_call(kernel, *, in_specs, out_specs, out_shape, **options):
    outs = [out_shape] if not isinstance(out_shape, list) else out_shape
    specs = [out_specs] if not isinstance(out_shape, list) else out_specs
    outs = [(pltpu.HBM if spec is HBM else pltpu.VMEM)(out.shape, out.dtype) for out, spec in zip(outs, specs)]
    call = pl.pallas_call(
        kernel,
        in_specs=in_specs,
        out_specs=out_specs,
        out_shape=outs if isinstance(out_shape, list) else outs[0],
        **options,
    )

    def run(*args):
        spaces = [pltpu.HBM if spec is HBM else pltpu.VMEM for spec in in_specs]
        return call(*[pltpu.with_memory_space_constraint(arg, space) for arg, space in zip(args, spaces)])

    return run


def call_lift(sz, feat, mat):
    return placed_call(
        functools.partial(lift_kernel, sz),
        in_specs=[VMEM, VMEM],
        out_specs=HBM,
        out_shape=shape_of(feat.shape[0], sz.flat, sz.cols),
        scratch_shapes=[pltpu.VMEM((2, sz.flat, sz.cols), BF16), sems(2)],
        compiler_params=params(),
        cost_estimate=cost(sz, feat.shape[0]),
        name="lift",
    )(feat, mat)


def call_own(sz, layer, back, a, point, tabs):
    return placed_call(
        functools.partial(own_kernel, sz, layer),
        in_specs=[VMEM, HBM, VMEM, HBM, HBM],
        out_specs=[HBM, VMEM, VMEM],
        out_shape=[shape_of(*a.shape), shape_of(sz.own, sz.flat, sz.slots), send_shape(sz)],
        scratch_shapes=streams(sz, max(sz.own, 2))
        + [
            pltpu.VMEM((sz.cols, sz.slots), BF16),
            square(sz.flat),
            square(sz.fwd, sz.chunk, sz.chans),
            square(sz.inv, sz.chunk, sz.chans),
            stage_f(sz),
            stage_i(sz),
            turned(sz),
        ],
        compiler_params=params(),
        cost_estimate=cost(sz, sz.own),
        name="own_field",
    )(back, a, point, tabs["gw"], tabs["fw"])


def call_unpack(sz, back):
    return placed_call(
        functools.partial(unpack_kernel, sz),
        in_specs=[VMEM],
        out_specs=VMEM,
        out_shape=shape_of(sz.own, sz.flat, sz.slots),
        scratch_shapes=[square(sz.flat), square(sz.inv, sz.chunk, sz.chans), stage_i(sz), turned(sz)],
        compiler_params=params(),
        cost_estimate=cost(sz, 1),
        name="unpack",
    )(back)


def call_rest(sz, layer, groups, zs, fields, point, tabs):
    count = sum(len(places) for places in groups)
    return placed_call(
        functools.partial(rest_kernel, sz, layer, groups),
        in_specs=[VMEM] * len(zs) + [HBM] * len(fields) + [VMEM, HBM],
        out_specs=[HBM] * len(fields),
        out_shape=[shape_of(*field.shape) for field in fields],
        scratch_shapes=streams(sz, count),
        compiler_params=params(),
        cost_estimate=cost(sz, count),
        name="rest_fields",
    )(*zs, *fields, point, tabs["gw"])


def call_final_own(sz, z, zs, fields, point, tabs):
    steps = sorted({step for step, _ in sz.halves[0]})
    zs = [zs[step - 1] for step in steps]
    return placed_call(
        functools.partial(final_own_kernel, sz, steps),
        in_specs=[VMEM] * (1 + len(zs)) + [HBM] * len(fields) + [VMEM, HBM],
        out_specs=[HBM, VMEM],
        out_shape=[shape_of(sz.micro, sz.flat, sz.cols), shape_of(len(sz.halves[1]), sz.flat, sz.cols)],
        scratch_shapes=streams(sz, sz.micro) + [pltpu.SemaphoreType.DMA],
        compiler_params=params(),
        cost_estimate=cost(sz, sz.own),
        name="final_own",
    )(z, *zs, *fields, point, tabs["gw"])


def call_final_rest(sz, zs, out, near, point, tabs):
    steps = sorted({step for step, _ in sz.halves[1]})
    zs = [zs[step - 1] for step in steps]
    return placed_call(
        functools.partial(final_rest_kernel, sz, steps),
        in_specs=[VMEM] * len(zs) + [HBM, VMEM, VMEM, HBM],
        out_specs=HBM,
        out_shape=shape_of(*out.shape),
        scratch_shapes=streams(sz, 2),
        input_output_aliases={len(zs): 0},
        compiler_params=params(),
        cost_estimate=cost(sz, len(zs) * sz.own),
        name="final_rest",
    )(*zs, out, near, point, tabs["gw"])


def call_split(sz, feats, weights, lift, point, bias):
    part = weights.shape[1:]
    message = shape_of(sz.modes * feats * part[2] + sz.note, part[3])
    outs = [shape_of(*part)] * (sz.section - 1) + [message] * sz.section
    made = placed_call(
        functools.partial(split_kernel, sz, feats),
        in_specs=[HBM] * 4,
        out_specs=[VMEM] * len(outs),
        out_shape=outs,
        scratch_shapes=[
            pltpu.VMEM(part, BF16),
            pltpu.VMEM(lift.shape, BF16),
            pltpu.VMEM(point.shape, BF16),
            pltpu.VMEM(bias.shape, BF16),
            pltpu.VMEM((feats, sz.chans, part[3]), F32),
            sems(sz.section + 3),
        ],
        compiler_params=params(),
        name="split",
    )(weights, lift, point, bias)
    return made[: sz.section - 1], made[sz.section - 1 :]


def call_cut(sz, weights, after):
    return placed_call(
        functools.partial(cut_kernel, sz),
        in_specs=[HBM, HBM],
        out_specs=[VMEM] * (sz.section - 2),
        out_shape=[shape_of(*weights.shape[1:])] * (sz.section - 2),
        scratch_shapes=[sems(sz.section - 2)],
        compiler_params=params(),
        name="cut",
    )(weights, after)


def call_first_mix(sz, feats, cols, messages, tabs):
    modes_h = tabs["eh"].shape[1] // 2
    return placed_call(
        functools.partial(first_mix_kernel, sz, feats),
        in_specs=[VMEM, VMEM, HBM] + [VMEM] * sz.section,
        out_specs=VMEM,
        out_shape=shape_of(sz.space, sz.section, 2, sz.rows, sz.inv * sz.chans),
        scratch_shapes=[
            pltpu.VMEM((cols.shape[0], 2 * modes_h), F32),
            pltpu.VMEM((sz.micro * sz.modes * sz.chans, 2 * modes_h), BF16),
            pltpu.VMEM((messages[0].shape[0] - sz.note, modes_h), F32),
            pltpu.VMEM(tabs["git"].shape, BF16),
            pltpu.SemaphoreType.DMA,
        ],
        compiler_params=params(),
        name="first_mix",
    )(cols, tabs["eh"], tabs["git"], *messages)


def call_pick(sz, layer, weights, parts, after):
    return placed_call(
        functools.partial(pick_kernel, sz, layer),
        in_specs=[HBM] * (sz.section + 1),
        out_specs=VMEM,
        out_shape=shape_of(*weights.shape[1:]),
        scratch_shapes=[pltpu.SemaphoreType.DMA],
        compiler_params=params(),
        name="pick",
    )(weights, *parts, after)


def call_mix(sz, recv, weights, tabs):
    modes_h = tabs["eh"].shape[1] // 2
    return placed_call(
        functools.partial(mix_kernel, sz),
        in_specs=[VMEM, VMEM, VMEM, HBM],
        out_specs=VMEM,
        out_shape=shape_of(sz.space, sz.section, 2, sz.rows, sz.inv * sz.chans),
        scratch_shapes=[
            pltpu.VMEM((sz.modes, sz.micro, 3, sz.chans, modes_h), F32),
            pltpu.VMEM((sz.micro * sz.modes * sz.chans, 2 * modes_h), BF16),
            pltpu.VMEM(tabs["git"].shape, BF16),
            pltpu.SemaphoreType.DMA,
        ],
        compiler_params=params(),
        cost_estimate=pl.CostEstimate(flops=4_000_000_000, bytes_accessed=2_000_000, transcendentals=0),
        name="mix",
    )(recv, weights, tabs["eh"], tabs["git"])


def exchange(value, count):
    return lax.all_to_all(value, BOTH, split_axis=0, concat_axis=0, tiled=True)


def tie(*values):
    return lax.optimization_barrier(values)


def swap(value, step, count, sources=None):
    pairs = [(i, i ^ step) for i in range(count) if sources is None or sources(i)]
    return lax.ppermute(value, "section", pairs)


def gather_last(value, count):
    last = count - 1
    return [lax.ppermute(value, "section", [(last ^ step, last)]) for step in range(1, count)]


def on_device(features, lift_w, spec_w, point_w, point_b):
    space = lax.axis_size("space")
    section = lax.axis_size("section")
    pos = lax.axis_index("section")
    micro, feats, rows, cols = features.shape
    chans = lift_w.shape[1]
    local = spec_w.shape[1]
    modes_h = spec_w.shape[2]
    modes_w = local * space
    height = rows * space
    modes = -(-local // section)
    spare = modes * section - local
    sz = Sizes(space, section, rows, chans, micro // section, modes, cols)

    order = mode_order(space, section, local, modes)
    known = (order >= 0)[:, None, :]
    slot = np.stack([2 * order, 2 * order + 1], axis=1) * known
    fw = np.where(known.reshape(1, modes, 1, -1), fwd_w_table(cols, modes_w).astype(np.float32)[:, slot], 0.0)
    gw = np.where(known[..., None], inv_w_table(cols, modes_w).astype(np.float32)[slot], 0.0)
    gw = gw.transpose(1, 0, 2, 3).reshape(sz.slots, cols)
    tabs = {
        "fw": fw.reshape(cols, sz.slots).astype(BF16),
        "gw": (0.5 * gw).astype(BF16),
        "eh": fwd_h_table(height, modes_h),
        "git": np.ascontiguousarray(inv_h_table(height, modes_h).T),
    }
    tabs = {name: jnp.asarray(table) for name, table in tabs.items()}

    weights = spec_w[0].transpose(0, 2, 3, 1)
    weights = jnp.pad(weights, ((0, spare), (0, 0), (0, 0), (0, 0)))
    weights = weights.reshape((section, modes) + weights.shape[1:])
    parts, messages = call_split(sz, feats, weights, lift_w, point_w, point_b)
    messages = [messages[0]] + [swap(messages[d], d, section) for d in range(1, section)]

    flat = features.reshape(section, sz.own, feats * rows, cols)
    mine = lax.dynamic_index_in_dim(flat, pos, 0, keepdims=False)
    send = jnp.einsum("mfrw,wk->kmfr", mine.reshape(sz.own, feats, rows, cols), tabs["fw"], preferred_element_type=F32)
    send = send.astype(BF16).reshape(sz.fwd, sz.devices, sz.own * feats * rows).transpose(1, 0, 2)
    recv = exchange(send, sz.devices).reshape(space, section, modes, 2, sz.own, feats, rows)
    recv = recv.transpose(1, 4, 2, 3, 5, 0, 6).reshape(micro * modes * 2 * feats, height)

    saved = [[None] * 3 for _ in range(section - 1)]
    for layer in range(section):
        if layer == 0:
            back = call_first_mix(sz, feats, recv, messages, tabs)
            back, flat, lift, *held = tie(back, flat, lift_w, *parts, *messages)
            point = jnp.stack([message[-sz.note :] for message in held[section - 1 :]], axis=0)
            near = swap(held[0], 1, section, lambda i: i > 0)
            held = [near] + [swap(held[d - 1], d, section, lambda i: 0 < i < section - 1) for d in range(2, section)]
        else:
            if layer == section - 1:
                held = last
            recv = exchange(send, sz.devices).reshape(space, section, sz.own, rows, sz.fwd * chans)
            if layer > 1:
                half, _ = tie(rest[1], send)
                rest[1] = call_rest(sz, layer - 2, sz.halves[1:], older, [half], point, tabs)[0]
                saved[layer - 2][2] = rest[1]
                recv, rest[1] = tie(recv, rest[1])
            picked = call_pick(sz, layer, weights, held, send)
            back = call_mix(sz, recv, picked, tabs)
            back, *zs = tie(back, *zs)
            zs += [swap(zs[steps.index(d - 1)], 1, section) for d in range(3, section, 2)]
            steps += range(3, section, 2)
            zs = [zs[steps.index(d)] for d in range(1, section)]
            back, *rest = tie(back, *rest)
            if layer == section - 2:
                far = call_cut(sz, weights, back)
                last = [near] + [swap(far[d - 2], d, section, lambda i: i == section - 1) for d in range(2, section)]
        back = exchange(back.reshape(sz.devices, 2, rows, sz.inv * chans), sz.devices)
        if layer == 0:
            feat = [lax.dynamic_index_in_dim(flat, pos ^ d, 0, keepdims=False) for d in range(section)]
            lift_mat = jnp.einsum("fc,rs->crfs", lift, jnp.eye(rows, dtype=BF16)).reshape(sz.flat, feats * rows)
            field = call_lift(sz, feat[0], lift_mat)
            feat = jnp.concatenate(feat[1:], axis=0)
            half = len(sz.halves[0])
            rest = [call_lift(sz, part, lift_mat) for part in (feat[:half], feat[half:])]
        elif layer < section - 1:
            rest[0] = call_rest(sz, layer - 1, sz.halves[:1], zs, rest[:1], point, tabs)[0]
            saved[layer - 1][1] = rest[0]
            older = zs
        else:
            rest = call_rest(sz, layer - 1, sz.halves, zs, rest, point, tabs)
            saved[layer - 1][1:] = rest
        back, *rest = tie(back, *rest)
        if layer + 1 < section:
            field, z, send = call_own(sz, layer, back, field, point, tabs)
            saved[layer][0] = field
            steps = [1] + list(range(2, section, 2))
            zs = [swap(z, d, section) for d in steps]
        else:
            z = call_unpack(sz, back)
            zs = gather_last(z, section)
            out, near = call_final_own(sz, z, zs, sum(saved, []), point, tabs)
            out = call_final_rest(sz, zs, out, near, point, tabs)
    return out.reshape(1, micro, chans, rows, cols)


def solution(mesh):
    in_specs = (
        P(None, None, "space", None),
        P(),
        P("section", "space", None, None, None),
        P("section", None, None),
        P("section", None),
    )
    out_specs = P("section", None, None, "space", None)
    return jax.shard_map(on_device, mesh=mesh, in_specs=in_specs, out_specs=out_specs, check_vma=False)
```

```python
import functools

import jax
import jax.numpy as jnp
import numpy as np
from jax import lax
from jax.experimental import pallas as pl
from jax.experimental.pallas import tpu as pltpu
from jax.sharding import PartitionSpec as P

BF16 = jnp.bfloat16
F32 = jnp.float32
BOTH = ("space", "section")


def turn_table(first, second, period):
    product = (first[:, None] * second[None, :]) % period
    return (np.float32(2.0 * np.pi) * product.astype(np.float32) / np.float32(period)).astype(np.float32)


def row_freqs(height, modes_h):
    index = np.arange(modes_h)
    return np.where(index < modes_h // 2, index, height - modes_h + index)


def mode_order(space, section, local, modes):
    part = np.arange(section)[None, None, :] * modes + np.arange(modes)[:, None, None]
    whole = np.arange(space)[None, :, None] * local + part
    return np.where(part < local, whole, -1).reshape(modes, space * section)


def fwd_w_table(cols, modes_w):
    slot = np.arange(2 * modes_w)
    angle = turn_table(np.arange(cols), slot // 2, cols)
    return np.where(slot[None, :] % 2 == 0, np.cos(angle), -np.sin(angle)).astype(BF16)


def fwd_h_table(height, modes_h):
    angle = turn_table(np.arange(height), row_freqs(height, modes_h), height)
    return np.concatenate([np.cos(angle), np.sin(angle)], axis=1).astype(BF16)


def inv_h_table(height, modes_h):
    angle = turn_table(row_freqs(height, modes_h), np.arange(height), height)
    cosine = np.cos(angle) / height
    sine = np.sin(angle) / height
    upper = np.concatenate([cosine, sine], axis=1)
    lower = np.concatenate([-sine, cosine], axis=1)
    return np.concatenate([upper, lower], axis=0).astype(BF16)


def inv_w_table(cols, modes_w):
    slot = np.arange(2 * modes_w)
    mode = slot // 2
    angle = turn_table(mode, np.arange(cols), cols)
    factor = np.where(mode == 0, 1.0, 2.0).astype(np.float32)[:, None] / cols
    return np.where(slot[:, None] % 2 == 0, factor * np.cos(angle), -factor * np.sin(angle)).astype(BF16)


def gelu(half):
    half = half.astype(BF16)
    inner = half * (BF16(1.5957691216057308) + BF16(0.2854192650890401) * (half * half))
    return half + half * jnp.tanh(inner)


def dot(left, right):
    return jnp.dot(left, right, preferred_element_type=F32)


def dot_tn(left, right):
    return lax.dot_general(left, right, (((0,), (0,)), ((), ())), preferred_element_type=F32)


def dot_nt(left, right):
    return lax.dot_general(left, right, (((1,), (1,)), ((), ())), preferred_element_type=F32)


class Sizes:
    def __init__(self, space, section, rows, chans, own, modes, cols):
        self.space, self.section, self.rows, self.chans = space, section, rows, chans
        self.own, self.modes, self.cols = own, modes, cols
        self.devices = space * section
        self.micro = own * section
        self.flat = chans * rows
        self.chunk = min(rows, max(1, 128 // chans))
        self.turns = rows // self.chunk
        self.fwd = 2 * modes
        self.inv = own * modes
        self.slots = 2 * modes * self.devices
        self.note = -(-(chans + 1) // 16) * 16
        others = [(step, m) for step in range(1, section) for m in range(own)]
        half = (len(others) + 1) // 3
        self.halves = [others[:half], others[half:]]
        self.step = min(512, cols)
        self.parts = cols // self.step


def iota(shape, axis):
    return lax.broadcasted_iota(jnp.int32, shape, axis)


def build_swap(ref, left, right, inner):
    size = left * right * inner
    row = iota((size, 1), 0)
    first, second, third = row // (right * inner), row // inner % right, row % inner
    target = (second * left + first) * inner + third
    ref[...] = jnp.where(iota((size, size), 1) == target, 1.0, 0.0).astype(BF16)


def build_mat(sz, layer, point_ref, mat_ref, bias_ref):
    pos = lax.axis_index("section")
    block = point_ref[pos ^ layer][:, : sz.chans] * BF16(0.5)
    expand = jnp.where(iota((sz.flat, sz.chans), 0) // sz.rows == iota((sz.flat, sz.chans), 1), 1.0, 0.0).astype(BF16)
    spread = dot_nt(expand, block[: sz.chans]).astype(BF16)
    full = dot_nt(spread, expand)
    same = iota((sz.flat, 1), 0) % sz.rows == iota((1, sz.flat), 1) % sz.rows
    mat_ref[...] = jnp.where(same, full, 0.0).astype(BF16)
    bias = jnp.broadcast_to(block[sz.chans : sz.chans + 1], (128, sz.chans))
    bias = jnp.where(iota(bias.shape, 0) == 0, bias.astype(F32), 0.0).astype(BF16)
    bias_ref[...] = dot_nt(expand, bias).astype(BF16)


def one_field(sz, z_ref, a_ref, mat_ref, bias_ref, gw_ref, out_ref, load, store):
    left = jnp.concatenate([mat_ref[...], z_ref[...], bias_ref[...]], axis=1)
    ones = jnp.ones((128, sz.step), BF16)
    for part in range(sz.cols // sz.step):
        cols = slice(part * sz.step, (part + 1) * sz.step)
        if part < len(load):
            load[part].wait()
        right = jnp.concatenate([a_ref[:, cols], gw_ref[:, cols], ones], axis=0)
        out_ref[:, cols] = gelu(dot(left, right))
        if store and (len(store) == sz.parts or part == sz.parts - 1):
            store[min(part, len(store) - 1)].start()


def pack(sz, field_ref, fw_ref, order_ref, swap_ref, stage_ref, send_ref):
    count, wide = sz.devices, sz.chunk * sz.chans
    spectra = [dot(field_ref[m], fw_ref[...]).astype(BF16) for m in range(sz.own)]
    turned = dot_tn(jnp.concatenate(spectra, axis=1), order_ref[...]).astype(BF16)
    blocks = []
    for m in range(sz.own):
        for t in range(sz.turns):
            lanes = slice(t * wide, (t + 1) * wide)
            starts = [m * sz.slots + k * count for k in range(sz.fwd)]
            blocks.append(jnp.concatenate([turned[start : start + count, lanes] for start in starts], axis=1))
    moved = dot(jnp.concatenate(blocks, axis=0), swap_ref[...])
    width = sz.fwd * sz.chans
    for i in range(sz.own * sz.turns):
        for r in range(sz.chunk):
            place = (i * sz.chunk + r) * count
            stage_ref[place : place + count, :] = moved[i * count : (i + 1) * count, r * width : (r + 1) * width]
    for m in range(sz.own):
        for device in range(count):
            piece = stage_ref[pl.ds(m * sz.rows * count + device, sz.rows, stride=count), :]
            send_ref[device, m] = piece.astype(BF16)


def unpack(sz, back_ref, order_ref, swap_ref, stage_ref, turned_ref, z_ref):
    count, wide = sz.devices, sz.chunk * sz.chans
    for q in range(2):
        for device in range(count):
            place = pl.ds(q * sz.rows * count + device, sz.rows, stride=count)
            stage_ref[place, :] = back_ref[device, q].astype(F32)
    blocks = []
    for i in range(2 * sz.turns):
        starts = [(i * sz.chunk + r) * count for r in range(sz.chunk)]
        blocks.append(jnp.concatenate([stage_ref[start : start + count, :] for start in starts], axis=1))
    moved = dot(jnp.concatenate(blocks, axis=0).astype(BF16), swap_ref[...]).astype(BF16)
    for q in range(2):
        for t in range(sz.turns):
            rows = slice((q * sz.turns + t) * count, (q * sz.turns + t + 1) * count)
            for k in range(sz.inv):
                m, mode = divmod(k, sz.modes)
                place = m * sz.slots + (q * sz.modes + mode) * count
                turned_ref[place : place + count, t * wide : (t + 1) * wide] = moved[rows, k * wide : (k + 1) * wide]
    spectra = dot_nt(order_ref[...], turned_ref[...]).astype(BF16)
    for m in range(sz.own):
        z_ref[m] = spectra[:, m * sz.slots : (m + 1) * sz.slots]


def copy_in(source, target, sem):
    copy = pltpu.make_async_copy(source, target, sem)
    copy.start()
    return copy


def copies(sz, source, target, sem, slot, cut):
    if not cut:
        return [pltpu.make_async_copy(source, target, sem.at[slot, 0])]
    made = []
    for part in range(sz.parts):
        cols = pl.ds(part * sz.step, sz.step)
        made.append(pltpu.make_async_copy(source.at[:, cols], target.at[:, cols], sem.at[slot, part]))
    return made


def lift_kernel(sz, feat_ref, mat_ref, out_ref, held_ref, out_sem):
    stores = []
    for i in range(feat_ref.shape[0]):
        if i >= 2:
            stores[i - 2].wait()
        held_ref[i % 2] = dot(mat_ref[...], feat_ref[i]).astype(BF16)
        stores.append(copy_in(held_ref.at[i % 2], out_ref.at[i], out_sem.at[i % 2]))
    for store in stores[-2:]:
        store.wait()


def own_kernel(sz, layer, back_ref, a_hbm, point_ref, gw_hbm, fw_hbm, out_ref, z_ref, send_ref, *scratch):
    (mat_ref, bias_ref, in_ref, held_ref, in_sem, out_sem, gw_ref, tab_sem,
     fw_ref, order_ref, swap_f_ref, swap_i_ref, stage_f_ref, stage_i_ref, turned_ref) = scratch
    gw_load = copy_in(gw_hbm, gw_ref, tab_sem.at[0])
    loads = [copies(sz, a_hbm.at[m], in_ref.at[m], in_sem, m, m == 0) for m in range(sz.own)]
    for copy in loads[0]:
        copy.start()
    build_swap(order_ref, sz.chans, sz.rows, 1)
    build_swap(swap_i_ref, sz.chunk, sz.inv, sz.chans)
    build_swap(swap_f_ref, sz.fwd, sz.chunk, sz.chans)
    build_mat(sz, layer, point_ref, mat_ref, bias_ref)
    unpack(sz, back_ref, order_ref, swap_i_ref, stage_i_ref, turned_ref, z_ref)
    for copy in sum(loads[1:], []):
        copy.start()
    fw_load = copy_in(fw_hbm, fw_ref, tab_sem.at[1])
    gw_load.wait()
    stores = []
    for m in range(sz.own):
        store = copies(sz, held_ref.at[m], out_ref.at[m], out_sem, m, False)
        one_field(sz, z_ref.at[m], in_ref.at[m], mat_ref, bias_ref, gw_ref, held_ref.at[m], loads[m], store)
        stores += store
    fw_load.wait()
    pack(sz, held_ref, fw_ref, order_ref, swap_f_ref, stage_f_ref, send_ref)
    for store in stores:
        store.wait()


def unpack_kernel(sz, back_ref, z_ref, order_ref, swap_ref, stage_ref, turned_ref):
    build_swap(order_ref, sz.chans, sz.rows, 1)
    build_swap(swap_ref, sz.chunk, sz.inv, sz.chans)
    unpack(sz, back_ref, order_ref, swap_ref, stage_ref, turned_ref, z_ref)


def run_fields(sz, layer, jobs, point_ref, gw_hbm, scratch):
    mat_ref, bias_ref, in_ref, held_ref, in_sem, out_sem, gw_ref, tab_sem = scratch
    gw_load = copy_in(gw_hbm, gw_ref, tab_sem.at[0])
    loads = [copies(sz, job[1], in_ref.at[i], in_sem, i, i == 0) for i, job in enumerate(jobs)]
    ahead = 2
    for copy in sum(loads[:ahead], []):
        copy.start()
    build_mat(sz, layer, point_ref, mat_ref, bias_ref)
    gw_load.wait()
    stores = []
    for i, (z_ref, _, target) in enumerate(jobs):
        if 0 < i and i + ahead - 1 < len(jobs):
            for copy in loads[i + ahead - 1]:
                copy.start()
        if i >= 2:
            for store in stores[i - 2]:
                store.wait()
        stores.append(copies(sz, held_ref.at[i % 2], target, out_sem, i % 2, i == len(jobs) - 1))
        one_field(sz, z_ref, in_ref.at[i], mat_ref, bias_ref, gw_ref, held_ref.at[i % 2], loads[i], stores[i])
    for store in sum(stores[-2:], []):
        store.wait()


def run_copies(jobs, scratch):
    _, _, in_ref, _, in_sem, out_sem, _, _ = scratch
    loads = [copy_in(source, in_ref.at[i], in_sem.at[i, 0]) for i, (source, _) in enumerate(jobs)]
    stores = []
    for i, (_, target) in enumerate(jobs):
        loads[i].wait()
        stores.append(copy_in(in_ref.at[i], target, out_sem.at[i, 0]))
    for store in stores:
        store.wait()


def rest_kernel(sz, layer, groups, *refs):
    count, parts = sz.section - 1, len(groups)
    z_refs, a_refs = refs[:count], refs[count : count + parts]
    point_ref, gw_hbm = refs[count + parts : count + parts + 2]
    out_refs, scratch = refs[count + parts + 2 : count + 2 * parts + 2], refs[count + 2 * parts + 2 :]
    jobs = []
    for places, a_ref, out_ref in zip(groups, a_refs, out_refs):
        for i, (step, m) in enumerate(places):
            jobs.append((z_refs[step - 1].at[m], a_ref.at[i], out_ref.at[i]))
    run_fields(sz, layer, jobs, point_ref, gw_hbm, scratch)


def final_own_kernel(sz, steps, z_ref, *refs):
    count = sz.section
    last = count - 1
    z_refs, refs = dict(zip(steps, refs)), refs[len(steps) :]
    fields = refs[: 3 * last]
    point_ref, gw_hbm, out_ref = refs[3 * last : 3 * last + 3]
    scratch = refs[3 * last + 3 :]
    pos = lax.axis_index("section")
    for layer in range(last):

        @pl.when(pos == layer)
        def _():
            own = [((layer * sz.own + m), fields[3 * layer].at[m]) for m in range(sz.own)]
            for half, places in enumerate(sz.halves):
                for i, (step, m) in enumerate(places):
                    own.append(((layer ^ step) * sz.own + m, fields[3 * layer + 1 + half].at[i]))
            run_copies([(place, out_ref.at[at]) for at, place in own], scratch)

    @pl.when(pos == last)
    def _():
        mine = fields[3 * last - 3]
        jobs = [(z_ref.at[m], mine.at[m], out_ref.at[last * sz.own + m]) for m in range(sz.own)]
        for i, (step, m) in enumerate(sz.halves[0]):
            jobs.append((z_refs[step].at[m], fields[3 * last - 2].at[i], out_ref.at[(last ^ step) * sz.own + m]))
        run_fields(sz, last, jobs, point_ref, gw_hbm, scratch)


def final_rest_kernel(sz, steps, *refs):
    last = sz.section - 1
    z_refs, refs = dict(zip(steps, refs)), refs[len(steps) :]
    _, rest_ref, point_ref, gw_hbm, out_ref = refs[:5]

    @pl.when(lax.axis_index("section") == last)
    def _():
        jobs = []
        for i, (step, m) in enumerate(sz.halves[1]):
            jobs.append((z_refs[step].at[m], rest_ref.at[i], out_ref.at[(last ^ step) * sz.own + m]))
        run_fields(sz, last, jobs, point_ref, gw_hbm, refs[5:])


def split_kernel(sz, feats, source_ref, lift_hbm, point_hbm, bias_hbm, *refs):
    count = sz.section
    part_refs = refs[: count - 1] + (refs[-6],)
    out_refs = refs[count - 1 : 2 * count - 1]
    lift_ref, point_ref, bias_ref, spread_ref, sem = refs[-5:]
    pos = lax.axis_index("section")
    small = [(lift_hbm, lift_ref), (point_hbm, point_ref), (bias_hbm, bias_ref)]
    small = [copy_in(source, target, sem.at[count + i]) for i, (source, target) in enumerate(small)]
    made = [copy_in(source_ref.at[pos ^ (d + 1) if d < count - 1 else pos], part_refs[d], sem.at[d]) for d in range(count)]
    for copy in small:
        copy.wait()
    square = (sz.chans, sz.chans)
    for f in range(feats):
        row = jnp.broadcast_to(lift_ref[f : f + 1].astype(F32), square)
        diagonal = jnp.where(iota(square, 0) == iota(square, 1), row, 0.0).astype(BF16)
        spread_ref[f] = dot(diagonal, jnp.ones((sz.chans, spread_ref.shape[2]), BF16))
    empty = jnp.zeros((sz.note - sz.chans - 1, sz.chans), F32)
    note = jnp.concatenate([point_ref[0].astype(F32), bias_ref[...].astype(F32), empty], axis=0).astype(BF16)
    for d in range(count):
        part_ref, out_ref = part_refs[d], out_refs[(d + 1) % count]
        made[d].wait()
        for mode in range(sz.modes):

            def body(c, accs):
                weight = part_ref[mode, c].astype(F32)
                return tuple(acc + spread_ref[f, pl.ds(c, 1), :] * weight for f, acc in enumerate(accs))

            zero = jnp.zeros(part_ref.shape[2:], F32)
            sums = lax.fori_loop(0, sz.chans, body, (zero,) * feats, unroll=4)
            for f in range(feats):
                size = zero.shape[0]
                at = (mode * feats + f) * size
                out_ref[at : at + size] = sums[f].astype(BF16)
        start = out_ref.shape[0] - sz.note
        out_ref[start:] = jnp.zeros((sz.note, out_ref.shape[1]), BF16)
        out_ref[start:, : sz.chans] = note


def cut_kernel(sz, source_ref, _, *refs):
    outs, sem = refs[:-1], refs[-1]
    pos = lax.axis_index("section")
    made = [copy_in(source_ref.at[pos ^ (i + 2)], out, sem.at[i]) for i, out in enumerate(outs)]
    for copy in made:
        copy.wait()


def pick_kernel(sz, layer, source_ref, *refs):
    parts, (_, out_ref, sem) = refs[:-3], refs[-3:]
    pos = lax.axis_index("section")
    for step in range(sz.section):

        @pl.when(pos == (layer ^ step))
        def _():
            source = parts[step - 1] if step else source_ref.at[layer]
            copy_in(source, out_ref, sem).wait()


def send_back(sz, git_ref, y_ref, out_ref):
    back = dot_nt(git_ref[...], y_ref[...]).astype(BF16)
    lanes = sz.inv * sz.chans
    height = sz.space * sz.rows
    for sp in range(sz.space):
        for dest in range(sz.section):
            for q in range(2):
                start = q * height + sp * sz.rows
                out_ref[sp, dest, q] = back[start : start + sz.rows, dest * lanes : (dest + 1) * lanes]


def first_mix_kernel(sz, feats, cols_ref, eh_ref, git_hbm, *refs):
    chans = sz.chans
    modes_h = eh_ref.shape[1] // 2
    messages = refs[: sz.section]
    out_ref, p_ref, y_ref, folded_ref, git_ref, sem = refs[sz.section :]
    load = copy_in(git_hbm, git_ref, sem)
    for step in range(sz.section):

        @pl.when(lax.axis_index("section") == step)
        def _():
            folded_ref[...] = messages[step][: folded_ref.shape[0]].astype(F32)

    p_ref[...] = dot(cols_ref[...], eh_ref[...])
    for mode in range(sz.modes):
        for m in range(sz.micro):
            out_re = jnp.zeros((chans, modes_h), F32)
            out_im = jnp.zeros((chans, modes_h), F32)
            for f in range(feats):
                at = (m * sz.modes + mode) * 2 * feats + f
                real, imag = p_ref[at : at + 1, :], p_ref[at + feats : at + feats + 1, :]
                x_re = real[:, :modes_h] + imag[:, modes_h:]
                x_im = imag[:, :modes_h] - real[:, modes_h:]
                at = (mode * feats + f) * 2 * chans
                w_re = folded_ref[at : at + chans, :]
                w_im = folded_ref[at + chans : at + 2 * chans, :]
                out_re += x_re * w_re - x_im * w_im
                out_im += x_re * w_im + x_im * w_re
            at = (m * sz.modes + mode) * chans
            y_ref[at : at + chans, :modes_h] = out_re.astype(BF16)
            y_ref[at : at + chans, modes_h:] = out_im.astype(BF16)
    load.wait()
    send_back(sz, git_ref, y_ref, out_ref)


def mix_kernel(sz, recv_ref, w_ref, eh_ref, git_hbm, out_ref, x_ref, y_ref, git_ref, sem):
    load = copy_in(git_hbm, git_ref, sem)
    modes_h = eh_ref.shape[1] // 2
    chans = sz.chans
    for src in range(sz.section):
        for m in range(sz.own):
            cols = recv_ref[:, src, m].reshape(sz.space * sz.rows, sz.fwd * chans)
            proj = dot_tn(cols, eh_ref[...])
            for mode in range(sz.modes):
                real = proj[2 * mode * chans : (2 * mode + 1) * chans]
                imag = proj[(2 * mode + 1) * chans : (2 * mode + 2) * chans]
                x_re = real[:, :modes_h] + imag[:, modes_h:]
                x_im = imag[:, :modes_h] - real[:, modes_h:]
                x_ref[mode, src * sz.own + m, 0] = x_re
                x_ref[mode, src * sz.own + m, 1] = x_im
                x_ref[mode, src * sz.own + m, 2] = x_re + x_im
    group = min(4, sz.micro)
    piece = 16 if chans % 16 == 0 else chans
    for mode in range(sz.modes):
        for base in range(0, sz.micro, group):
            for first in range(0, chans, piece):

                def body(c, accs):
                    w_re = w_ref[mode, c, first : first + piece].astype(F32)
                    w_im = w_ref[mode, c, chans + first : chans + first + piece].astype(F32)
                    less, more = w_im - w_re, w_im + w_re
                    new = []
                    for g in range(group):
                        x_re, x_im, x_sum = (x_ref[mode, base + g, part, pl.ds(c, 1), :] for part in range(3))
                        both, second, third = accs[3 * g : 3 * g + 3]
                        new += [both + x_sum * w_re, second + x_re * less, third + x_im * more]
                    return tuple(new)

                zero = jnp.zeros((piece, modes_h), F32)
                accs = lax.fori_loop(0, chans, body, (zero,) * (3 * group), unroll=8)
                for g in range(group):
                    both, second, third = accs[3 * g : 3 * g + 3]
                    at = ((base + g) * sz.modes + mode) * chans + first
                    y_ref[at : at + piece, :modes_h] = (both - third).astype(BF16)
                    y_ref[at : at + piece, modes_h:] = (both + second).astype(BF16)
    load.wait()
    send_back(sz, git_ref, y_ref, out_ref)


HBM = pl.BlockSpec(memory_space=pltpu.HBM)
VMEM = pl.BlockSpec(memory_space=pltpu.VMEM)


def params(size=30):
    return pltpu.CompilerParams(vmem_limit_bytes=size * 1024 * 1024)


def cost(sz, fields, extra=0):
    return pl.CostEstimate(
        flops=fields * 2 * sz.flat * sz.cols * (sz.flat + 256) + extra,
        bytes_accessed=fields * 4 * sz.flat * sz.cols,
        transcendentals=fields * sz.flat * sz.cols,
    )


def shape_of(*shape, dtype=BF16):
    return jax.ShapeDtypeStruct(shape, dtype)


def stage_f(sz):
    return pltpu.VMEM((sz.own * sz.rows * sz.devices, sz.fwd * sz.chans), F32)


def stage_i(sz):
    return pltpu.VMEM((2 * sz.rows * sz.devices, sz.inv * sz.chans), F32)


def turned(sz):
    return pltpu.VMEM((sz.own * sz.slots, sz.flat), BF16)


def send_shape(sz):
    return shape_of(sz.devices, sz.own, sz.rows, sz.fwd * sz.chans)


def square(*sizes):
    size = int(np.prod(sizes))
    return pltpu.VMEM((size, size), BF16)


def sems(*counts):
    return pltpu.SemaphoreType.DMA(counts)


def streams(sz, jobs):
    return [
        square(sz.flat),
        pltpu.VMEM((sz.flat, 128), BF16),
        pltpu.VMEM((jobs, sz.flat, sz.cols), BF16),
        pltpu.VMEM((2, sz.flat, sz.cols), BF16),
        sems(jobs, sz.parts),
        sems(jobs, sz.parts),
        pltpu.VMEM((sz.slots, sz.cols), BF16),
        sems(2),
    ]


def placed_call(kernel, *, in_specs, out_specs, out_shape, **options):
    outs = [out_shape] if not isinstance(out_shape, list) else out_shape
    specs = [out_specs] if not isinstance(out_shape, list) else out_specs
    outs = [(pltpu.HBM if spec is HBM else pltpu.VMEM)(out.shape, out.dtype) for out, spec in zip(outs, specs)]
    call = pl.pallas_call(
        kernel,
        in_specs=in_specs,
        out_specs=out_specs,
        out_shape=outs if isinstance(out_shape, list) else outs[0],
        **options,
    )

    def run(*args):
        spaces = [pltpu.HBM if spec is HBM else pltpu.VMEM for spec in in_specs]
        return call(*[pltpu.with_memory_space_constraint(arg, space) for arg, space in zip(args, spaces)])

    return run


def call_lift(sz, feat, mat):
    return placed_call(
        functools.partial(lift_kernel, sz),
        in_specs=[VMEM, VMEM],
        out_specs=HBM,
        out_shape=shape_of(feat.shape[0], sz.flat, sz.cols),
        scratch_shapes=[pltpu.VMEM((2, sz.flat, sz.cols), BF16), sems(2)],
        compiler_params=params(),
        cost_estimate=cost(sz, feat.shape[0]),
        name="lift",
    )(feat, mat)


def call_own(sz, layer, back, a, point, tabs):
    return placed_call(
        functools.partial(own_kernel, sz, layer),
        in_specs=[VMEM, HBM, VMEM, HBM, HBM],
        out_specs=[HBM, VMEM, VMEM],
        out_shape=[shape_of(*a.shape), shape_of(sz.own, sz.flat, sz.slots), send_shape(sz)],
        scratch_shapes=streams(sz, max(sz.own, 2))
        + [
            pltpu.VMEM((sz.cols, sz.slots), BF16),
            square(sz.flat),
            square(sz.fwd, sz.chunk, sz.chans),
            square(sz.inv, sz.chunk, sz.chans),
            stage_f(sz),
            stage_i(sz),
            turned(sz),
        ],
        compiler_params=params(),
        cost_estimate=cost(sz, sz.own),
        name="own_field",
    )(back, a, point, tabs["gw"], tabs["fw"])


def call_unpack(sz, back):
    return placed_call(
        functools.partial(unpack_kernel, sz),
        in_specs=[VMEM],
        out_specs=VMEM,
        out_shape=shape_of(sz.own, sz.flat, sz.slots),
        scratch_shapes=[square(sz.flat), square(sz.inv, sz.chunk, sz.chans), stage_i(sz), turned(sz)],
        compiler_params=params(),
        cost_estimate=cost(sz, 1),
        name="unpack",
    )(back)


def call_rest(sz, layer, groups, zs, fields, point, tabs):
    count = sum(len(places) for places in groups)
    return placed_call(
        functools.partial(rest_kernel, sz, layer, groups),
        in_specs=[VMEM] * len(zs) + [HBM] * len(fields) + [VMEM, HBM],
        out_specs=[HBM] * len(fields),
        out_shape=[shape_of(*field.shape) for field in fields],
        scratch_shapes=streams(sz, count),
        compiler_params=params(),
        cost_estimate=cost(sz, count),
        name="rest_fields",
    )(*zs, *fields, point, tabs["gw"])


def call_final_own(sz, z, zs, fields, point, tabs):
    steps = sorted({step for step, _ in sz.halves[0]})
    zs = [zs[step - 1] for step in steps]
    return placed_call(
        functools.partial(final_own_kernel, sz, steps),
        in_specs=[VMEM] * (1 + len(zs)) + [HBM] * len(fields) + [VMEM, HBM],
        out_specs=HBM,
        out_shape=shape_of(sz.micro, sz.flat, sz.cols),
        scratch_shapes=streams(sz, sz.micro),
        compiler_params=params(),
        cost_estimate=cost(sz, sz.own),
        name="final_own",
    )(z, *zs, *fields, point, tabs["gw"])


def call_final_rest(sz, zs, out, rest, point, tabs):
    steps = sorted({step for step, _ in sz.halves[1]})
    zs = [zs[step - 1] for step in steps]
    return placed_call(
        functools.partial(final_rest_kernel, sz, steps),
        in_specs=[VMEM] * len(zs) + [HBM, HBM, VMEM, HBM],
        out_specs=HBM,
        out_shape=shape_of(*out.shape),
        scratch_shapes=streams(sz, len(sz.halves[1])),
        input_output_aliases={len(zs): 0},
        compiler_params=params(),
        cost_estimate=cost(sz, len(zs) * sz.own),
        name="final_rest",
    )(*zs, out, rest, point, tabs["gw"])


def call_split(sz, feats, weights, lift, point, bias):
    part = weights.shape[1:]
    message = shape_of(sz.modes * feats * part[2] + sz.note, part[3])
    outs = [shape_of(*part)] * (sz.section - 1) + [message] * sz.section
    made = placed_call(
        functools.partial(split_kernel, sz, feats),
        in_specs=[HBM] * 4,
        out_specs=[VMEM] * len(outs),
        out_shape=outs,
        scratch_shapes=[
            pltpu.VMEM(part, BF16),
            pltpu.VMEM(lift.shape, BF16),
            pltpu.VMEM(point.shape, BF16),
            pltpu.VMEM(bias.shape, BF16),
            pltpu.VMEM((feats, sz.chans, part[3]), F32),
            sems(sz.section + 3),
        ],
        compiler_params=params(),
        name="split",
    )(weights, lift, point, bias)
    return made[: sz.section - 1], made[sz.section - 1 :]


def call_cut(sz, weights, after):
    return placed_call(
        functools.partial(cut_kernel, sz),
        in_specs=[HBM, HBM],
        out_specs=[VMEM] * (sz.section - 2),
        out_shape=[shape_of(*weights.shape[1:])] * (sz.section - 2),
        scratch_shapes=[sems(sz.section - 2)],
        compiler_params=params(),
        name="cut",
    )(weights, after)


def call_first_mix(sz, feats, cols, messages, tabs):
    modes_h = tabs["eh"].shape[1] // 2
    return placed_call(
        functools.partial(first_mix_kernel, sz, feats),
        in_specs=[VMEM, VMEM, HBM] + [VMEM] * sz.section,
        out_specs=VMEM,
        out_shape=shape_of(sz.space, sz.section, 2, sz.rows, sz.inv * sz.chans),
        scratch_shapes=[
            pltpu.VMEM((cols.shape[0], 2 * modes_h), F32),
            pltpu.VMEM((sz.micro * sz.modes * sz.chans, 2 * modes_h), BF16),
            pltpu.VMEM((messages[0].shape[0] - sz.note, modes_h), F32),
            pltpu.VMEM(tabs["git"].shape, BF16),
            pltpu.SemaphoreType.DMA,
        ],
        compiler_params=params(),
        name="first_mix",
    )(cols, tabs["eh"], tabs["git"], *messages)


def call_pick(sz, layer, weights, parts, after):
    return placed_call(
        functools.partial(pick_kernel, sz, layer),
        in_specs=[HBM] * (sz.section + 1),
        out_specs=VMEM,
        out_shape=shape_of(*weights.shape[1:]),
        scratch_shapes=[pltpu.SemaphoreType.DMA],
        compiler_params=params(),
        name="pick",
    )(weights, *parts, after)


def call_mix(sz, recv, weights, tabs):
    modes_h = tabs["eh"].shape[1] // 2
    return placed_call(
        functools.partial(mix_kernel, sz),
        in_specs=[VMEM, VMEM, VMEM, HBM],
        out_specs=VMEM,
        out_shape=shape_of(sz.space, sz.section, 2, sz.rows, sz.inv * sz.chans),
        scratch_shapes=[
            pltpu.VMEM((sz.modes, sz.micro, 3, sz.chans, modes_h), F32),
            pltpu.VMEM((sz.micro * sz.modes * sz.chans, 2 * modes_h), BF16),
            pltpu.VMEM(tabs["git"].shape, BF16),
            pltpu.SemaphoreType.DMA,
        ],
        compiler_params=params(),
        cost_estimate=pl.CostEstimate(flops=4_000_000_000, bytes_accessed=2_000_000, transcendentals=0),
        name="mix",
    )(recv, weights, tabs["eh"], tabs["git"])


def exchange(value, count):
    return lax.all_to_all(value, BOTH, split_axis=0, concat_axis=0, tiled=True)


def tie(*values):
    return lax.optimization_barrier(values)


def swap(value, step, count, sources=None):
    pairs = [(i, i ^ step) for i in range(count) if sources is None or sources(i)]
    return lax.ppermute(value, "section", pairs)


def gather_last(value, count):
    last = count - 1
    far = [lax.ppermute(value, "section", [(last ^ step, last)]) for step in range(2, count)]
    return [swap(value, 1, count)] + far


def on_device(features, lift_w, spec_w, point_w, point_b):
    space = lax.axis_size("space")
    section = lax.axis_size("section")
    pos = lax.axis_index("section")
    micro, feats, rows, cols = features.shape
    chans = lift_w.shape[1]
    local = spec_w.shape[1]
    modes_h = spec_w.shape[2]
    modes_w = local * space
    height = rows * space
    modes = -(-local // section)
    spare = modes * section - local
    sz = Sizes(space, section, rows, chans, micro // section, modes, cols)

    order = mode_order(space, section, local, modes)
    known = (order >= 0)[:, None, :]
    slot = np.stack([2 * order, 2 * order + 1], axis=1) * known
    fw = np.where(known.reshape(1, modes, 1, -1), fwd_w_table(cols, modes_w).astype(np.float32)[:, slot], 0.0)
    gw = np.where(known[..., None], inv_w_table(cols, modes_w).astype(np.float32)[slot], 0.0)
    gw = gw.transpose(1, 0, 2, 3).reshape(sz.slots, cols)
    tabs = {
        "fw": fw.reshape(cols, sz.slots).astype(BF16),
        "gw": (0.5 * gw).astype(BF16),
        "eh": fwd_h_table(height, modes_h),
        "git": np.ascontiguousarray(inv_h_table(height, modes_h).T),
    }
    tabs = {name: jnp.asarray(table) for name, table in tabs.items()}

    weights = spec_w[0].transpose(0, 2, 3, 1)
    weights = jnp.pad(weights, ((0, spare), (0, 0), (0, 0), (0, 0)))
    weights = weights.reshape((section, modes) + weights.shape[1:])
    parts, messages = call_split(sz, feats, weights, lift_w, point_w, point_b)
    messages = [messages[0]] + [swap(messages[d], d, section) for d in range(1, section)]

    flat = features.reshape(section, sz.own, feats * rows, cols)
    mine = lax.dynamic_index_in_dim(flat, pos, 0, keepdims=False)
    send = jnp.einsum("mfrw,wk->kmfr", mine.reshape(sz.own, feats, rows, cols), tabs["fw"], preferred_element_type=F32)
    send = send.astype(BF16).reshape(sz.fwd, sz.devices, sz.own * feats * rows).transpose(1, 0, 2)
    recv = exchange(send, sz.devices).reshape(space, section, modes, 2, sz.own, feats, rows)
    recv = recv.transpose(1, 4, 2, 3, 5, 0, 6).reshape(micro * modes * 2 * feats, height)

    saved = [[None] * 3 for _ in range(section - 1)]
    for layer in range(section):
        if layer == 0:
            back = call_first_mix(sz, feats, recv, messages, tabs)
            back, flat, lift, *held = tie(back, flat, lift_w, *parts, *messages)
            point = jnp.stack([message[-sz.note :] for message in held[section - 1 :]], axis=0)
            near = swap(held[0], 1, section, lambda i: i > 0)
            held = [near] + [swap(held[d - 1], d, section, lambda i: 0 < i < section - 1) for d in range(2, section)]
        else:
            if layer == section - 1:
                held = last
            recv = exchange(send, sz.devices).reshape(space, section, sz.own, rows, sz.fwd * chans)
            if layer == 1:
                recv, *rest = tie(recv, *rest)
            else:
                half, _ = tie(rest[1], send)
                rest[1] = call_rest(sz, layer - 2, sz.halves[1:], older, [half], point, tabs)[0]
                saved[layer - 2][2] = rest[1]
                recv, rest[1] = tie(recv, rest[1])
            picked = call_pick(sz, layer, weights, held, send)
            back = call_mix(sz, recv, picked, tabs)
            back, *zs = tie(back, *zs)
            zs += [swap(zs[steps.index(d - 1)], 1, section) for d in range(3, section, 2)]
            steps += range(3, section, 2)
            zs = [zs[steps.index(d)] for d in range(1, section)]
            back, *rest = tie(back, *rest)
            if layer == section - 2:
                far = call_cut(sz, weights, back)
                last = [near] + [swap(far[d - 2], d, section, lambda i: i == section - 1) for d in range(2, section)]
        back = exchange(back.reshape(sz.devices, 2, rows, sz.inv * chans), sz.devices)
        if layer == 0:
            lift_mat = jnp.einsum("fc,rs->crfs", lift, jnp.eye(rows, dtype=BF16)).reshape(sz.flat, feats * rows)
            field = call_lift(sz, lax.dynamic_index_in_dim(flat, pos, 0, keepdims=False), lift_mat)
            rest = []
        elif layer < section - 1:
            rest[0] = call_rest(sz, layer - 1, sz.halves[:1], zs, rest[:1], point, tabs)[0]
            saved[layer - 1][1] = rest[0]
            older = zs
        else:
            rest = call_rest(sz, layer - 1, sz.halves, zs, rest, point, tabs)
            saved[layer - 1][1:] = rest
        back, *rest = tie(back, *rest)
        if layer + 1 < section:
            field, z, send = call_own(sz, layer, back, field, point, tabs)
            saved[layer][0] = field
            steps = [1] + list(range(2, section, 2))
            zs = [swap(z, d, section) for d in steps]
            if layer == 0:
                flat, _ = tie(flat, send)
                feat = [lax.dynamic_index_in_dim(flat, pos ^ d, 0, keepdims=False) for d in range(1, section)]
                feat = jnp.concatenate(feat, axis=0)
                half = len(sz.halves[0])
                rest = [call_lift(sz, part, lift_mat) for part in (feat[:half], feat[half:])]
        else:
            z = call_unpack(sz, back)
            zs = gather_last(z, section)
            out = call_final_own(sz, z, zs, sum(saved, []), point, tabs)
            out = call_final_rest(sz, zs, out, rest[1], point, tabs)
    return out.reshape(1, micro, chans, rows, cols)


def solution(mesh):
    in_specs = (
        P(None, None, "space", None),
        P(),
        P("section", "space", None, None, None),
        P("section", None, None),
        P("section", None),
    )
    out_specs = P("section", None, None, "space", None)
    return jax.shard_map(on_device, mesh=mesh, in_specs=in_specs, out_specs=out_specs, check_vma=False)
```
